128 devices in a mesh: pw: 16 (over z, y), band: 8 (over x, core).
Axes of the slice: x: 4, y: 4, z: 4, core: 2. Of those that a mesh axis runs over, the one named last changes fastest.
Arguments:
- coefficients: float32 [128, 393216], P(None, ('pw', 'band')), may hold values from -24 to 24
- occupancy: float32 [128], replicated, may hold values from 0.5 to 2
- kinetic: float32 [393216], P(('pw', 'band')), may hold values from 0.1 to 3
- cell_map: int32 [393216], P('pw'), may hold values from 0 to 884735, as said below
- potential_ext: float32 [96, 9216], P('pw'), may hold values from -6 to 6
- core_density: float32 [96, 9216], P('pw'), may hold values from 0.2 to 1
Outputs:
- grad_coef: float32 [128, 393216], P(None, ('pw', 'band'))
- density: float32 [96, 9216], P('pw')
The draws below stay inside these ranges and needn't reach their ends.
Inputs may be any that keep to these rules, and one draw needn't show every extreme that they name: `cell_map`: positions p * 24576 to (p + 1) * 24576 - 1 hold distinct cell numbers whose y lies from p * 6 to (p + 1) * 6 - 1; each such block holds the first and the last cell of its planes.
All inputs are finite; a program needn't handle non-finite values.
Results may differ from the reference program's by a relative error of at most 0.0003.
Values sent between devices are 32-bit elements; how exact they have to be, the bound alone decides.
No kernel may reach another device: no remote copies, remote signals or barrier semaphores. Data moves between devices by JAX's collectives and lax.ppermute only.
A program may use at most 128 MiB of HBM per device.

```python
import math
import jax
import jax.numpy as jnp
from jax import lax

G = 96
NPW = 393216
NB = 128
NS_ITERS = 4
GY = 6
PW_DEV = 24576


def draw_coefficients(key, part):
    key_base, key_scale = jax.random.split(key)
    widths = jax.random.uniform(key_scale, (NB,), jnp.float32, 0.0, 1.0)
    base_values = jax.random.truncated_normal(key_base, -4.0, 4.0, (NB, NPW), jnp.float32)
    column_scale = jnp.exp(widths * math.log(3.2))
    mixed_values = base_values + 0.5 * jnp.roll(base_values, -1, axis=0) + 0.3 * jnp.roll(base_values, -7, axis=0)
    return column_scale[:, None] * mixed_values


def draw_cell_map(key, part):
    slab_cells = GY * G * G
    per_dev = PW_DEV

    def one_block(position):
        block_key = jax.random.fold_in(key, position)
        first_key, second_key = jax.random.split(block_key)
        middle_cells = jax.random.permutation(first_key, slab_cells - 2)[:per_dev - 2].astype(jnp.int32) + 1
        chosen = jnp.concatenate([jnp.zeros((1,), jnp.int32), jnp.full((1,), slab_cells - 1, jnp.int32), middle_cells])
        return jax.random.permutation(second_key, chosen) + position * slab_cells
    return jax.vmap(one_block)(jnp.arange(NPW // PW_DEV, dtype=jnp.int32)).reshape(NPW)


def block_levels(rng, dims, cuts, low, largest):
    loudness, own = 1.0, jax.random.fold_in(rng, 6)
    for axis_at, shards_of in cuts:
        steps = jnp.exp(jax.random.uniform(jax.random.fold_in(own, axis_at), (shards_of,), jnp.float32, low / len(cuts), largest / len(cuts)))
        loudness = loudness * jnp.repeat(steps, dims[axis_at] // shards_of).reshape([-1 if axis == axis_at else 1 for axis in range(len(dims))])
    return loudness


def noise(rng, shape, width, bound, cuts=(), kind=jnp.bfloat16):
    entries = width * jax.random.normal(rng, shape, jnp.float32)
    if cuts:
        entries = entries * block_levels(rng, shape, cuts, -0.22, 0.18)
    return jnp.clip(entries, -bound, bound).astype(kind)


def setup_inputs(seed: int = 0) -> dict:
    seeds = jax.random.split(jax.random.key(seed), 7)
    coefficients = draw_coefficients(jax.random.fold_in(seeds[6], 71), 0)
    occupancy = jnp.clip(jnp.exp(jax.random.uniform(seeds[1], (NB,), jnp.float32, math.log(0.5), math.log(2.0))), 0.5, 2.0)
    kinetic = jnp.clip(jnp.exp(math.log(3.0) - 3.4011974 * jax.random.uniform(seeds[2], (NPW,), jnp.float32) ** block_levels(seeds[2], (NPW,), ((0, 128),), -0.2, 0.2)), 0.1, 3.0)
    cell_map = draw_cell_map(jax.random.fold_in(seeds[6], 71), 0)
    potential_ext = noise(seeds[4], (G, G * G), 1.0, 6.0, ((0, 16),), jnp.float32)
    core_density = jnp.clip(jnp.exp(math.log(1.0) - 1.609438 * jax.random.uniform(seeds[5], (G, G * G), jnp.float32) ** block_levels(seeds[5], (G, G * G), ((0, 16),), -0.2, 0.2)), 0.2, 1.0)
    return dict(coefficients=coefficients, occupancy=occupancy, kinetic=kinetic, cell_map=cell_map, potential_ext=potential_ext, core_density=core_density)


highest = lax.Precision.HIGHEST
slater = 0.9847450218426965

def cas_table(length):
    counter = jnp.arange(length, dtype=jnp.int32)
    product = counter[:, None] * counter[None, :] % length
    phases = product.astype(jnp.float32) * (2.0 * math.pi / length)
    return jnp.cos(phases) + jnp.sin(phases)

def matmul(left_side, right_side):
    return jnp.dot(left_side, right_side, precision=highest, preferred_element_type=jnp.float32)

def along_axis(values, cas_values, pattern):
    return jnp.einsum(pattern, values, cas_values, precision=highest, preferred_element_type=jnp.float32)

def loewdin(intersection):
    frob_norm = jnp.sqrt(jnp.sum(intersection * intersection))
    identity = jnp.eye(intersection.shape[0], dtype=jnp.float32)
    y_iter = intersection / frob_norm
    z_iter = identity
    for repeat in range(NS_ITERS):
        middle = 1.5 * identity - 0.5 * matmul(z_iter, y_iter)
        y_iter = matmul(y_iter, middle)
        z_iter = matmul(middle, z_iter)
    return z_iter / jnp.sqrt(frob_norm)

def to_fields(coeffs, cell_map, cas_values):
    members = coeffs.shape[0]
    placed = jnp.zeros((members, G * G * G), jnp.float32).at[:, cell_map].set(coeffs)
    shaped = placed.reshape(members, G, G, G)
    shaped = along_axis(shaped, cas_values, 'byxz,zk->byxk')
    shaped = jnp.transpose(shaped, (0, 3, 1, 2))
    shaped = along_axis(shaped, cas_values, 'bzyx,yk->bzkx')
    shaped = along_axis(shaped, cas_values, 'bzyx,xk->bzyk')
    return shaped.reshape(members, G, G * G)

def from_fields(product, cell_map, cas_values, inv_root):
    members = product.shape[0]
    shaped = product.reshape(members, G, G, G)
    shaped = along_axis(shaped, cas_values, 'bzyx,xk->bzyk')
    shaped = along_axis(shaped, cas_values, 'bzyx,yk->bzkx')
    shaped = jnp.transpose(shaped, (0, 2, 3, 1))
    shaped = along_axis(shaped, cas_values, 'byxz,zk->byxk')
    return shaped.reshape(members, G * G * G)[:, cell_map] * inv_root

def reference(coefficients, occupancy, kinetic, cell_map, potential_ext, core_density):
    cas_values = cas_table(G)
    inv_root = 1.0 / math.sqrt(NPW)
    intersection = matmul(coefficients, coefficients.T) / NPW
    weights, pullback = jax.vjp(loewdin, intersection)
    rotated = matmul(weights.T, coefficients)
    spread = rotated * inv_root
    band_share = occupancy / NB
    block_rows = 32
    blocks = NB // block_rows
    spread_blocks = spread.reshape(blocks, block_rows, NPW)
    share_blocks = band_share.reshape(blocks, block_rows)

    def add_block(running, pieces):
        fields = to_fields(pieces[0], cell_map, cas_values)
        return (running + lax.optimization_barrier(jnp.sum(pieces[1][:, None, None] * fields * fields, axis=0)), None)
    summed, unused = lax.scan(add_block, jnp.zeros((G, G * G), jnp.float32), (spread_blocks, share_blocks))
    density = core_density + summed
    potential = potential_ext - slater * jnp.cbrt(density)

    def grid_block(coeffs):
        fields = to_fields(coeffs, cell_map, cas_values)
        return from_fields(potential[None] * fields, cell_map, cas_values, inv_root)
    grid_term = lax.map(grid_block, spread_blocks).reshape(NB, NPW)
    grad_rotated = occupancy[:, None] * (kinetic[None, :] * rotated + grid_term)
    grad_weights = matmul(coefficients, grad_rotated.T)
    grad_intersection, = pullback(grad_weights)
    grad_coef = matmul(weights, grad_rotated) + matmul(grad_intersection + grad_intersection.T, coefficients) / NPW
    return (grad_coef, density)
```

```python
import math

import jax
import jax.numpy as jnp
import ml_dtypes
import numpy as np
from jax import lax
from jax.experimental import pallas as pl
from jax.experimental.pallas import tpu as pltpu
from jax.sharding import PartitionSpec as P

G = 96
NPW = 393216
NB = 128
NS_ITERS = 4
PW = 16
BD = 8
LB = NB // BD
GY = G // PW
COLS = G * G // (G * BD) * GY
SLAB = GY * G * G
KW = NPW // (PW * BD)
BLK = GY * COLS
ROWS = PW * BLK
SUM_ROWS = ROWS // LB
LANES = 128

highest = lax.Precision.HIGHEST
slater = 0.9847450218426965
bf16 = jnp.bfloat16
f32 = jnp.float32


def halves(table):
    high = table.astype(ml_dtypes.bfloat16)
    low = (table - high.astype(np.float64)).astype(ml_dtypes.bfloat16)
    return high, low


def tables():
    counter = np.arange(G)
    phases = 2.0 * np.pi / G * (counter[:, None] * counter[None, :] % G)
    cas = np.cos(phases) + np.sin(phases)
    order = (np.arange(PW)[None, :] * GY + np.arange(GY)[:, None]).reshape(-1)
    scaled = cas / math.sqrt(NPW)
    mixes = []
    small = np.arange(8)

    def mix(m):
        beta = 2.0 * np.pi / G * (small[:, None] * (m + 12 * small[None, :]))
        even = np.kron(np.cos(beta) + np.sin(beta), np.eye(LB))
        odd = np.kron(np.cos(beta) - np.sin(beta), np.eye(LB))
        return even, odd

    zero = np.zeros((LANES, LANES))
    mixes.append(np.block([[mix(0)[0], zero], [zero, mix(6)[0]]]))
    for m in range(1, 6):
        here, there = mix(m), mix(12 - m)
        mixes.append(np.block([[here[0], there[0]], [here[1], -there[1]]]))
    mixes = np.stack(mixes)
    return dict(
        z_out=halves(scaled[order, :]),
        y_out=halves(cas[:, order]),
        y_in=halves(cas[order, :]),
        z_in=halves(scaled[:, order]),
        mix=halves(mixes),
        mix_t=halves(np.swapaxes(mixes, 1, 2)),
    )


ROOT3 = math.sqrt(3.0) / 2.0


def cos12(e):
    a0, a1, a2 = e[0] + e[6], e[1] + e[5], e[2] + e[4]
    b0, b1, b2 = e[0] - e[6], e[1] - e[5], e[2] - e[4]
    t = ROOT3 * b1
    h = b0 + 0.5 * b2
    r = 0.5 * (a1 + a2)
    d = 0.5 * (a1 - a2)
    return [
        a0 + a1 + a2 + e[3],
        h + t,
        a0 + d - e[3],
        b0 - b2,
        a0 - r + e[3],
        h - t,
        a0 - a1 + a2 - e[3],
    ]


def sin12(o):
    p1, p2 = o[1] + o[5], o[2] + o[4]
    r1, r2 = o[1] - o[5], o[2] - o[4]
    h = 0.5 * p1 + o[3]
    t = ROOT3 * p2
    return [None, h + t, ROOT3 * (r1 + r2), p1 - o[3], ROOT3 * (r1 - r2), h - t]


def split(values):
    high = values.astype(bf16)
    return high, (values - high.astype(f32)).astype(bf16)


def dot(a, b):
    return jnp.dot(a, b, preferred_element_type=f32)


def dot3(a, b):
    return dot(a[0], b[0]) + (dot(a[0], b[1]) + dot(a[1], b[0]))


def lane_bit(shape, bit):
    return (lax.broadcasted_iota(jnp.int32, shape, 1) & bit) == 0


def gather_groups(parts, shape):
    for width in (16, 32, 64):
        first = lane_bit(shape, width)
        parts = [
            jnp.where(first, a, b) + pltpu.roll(jnp.where(first, b, a), width, 1)
            for a, b in zip(parts[0::2], parts[1::2])
        ]
    return parts[0]


def spread_groups(value, shape):
    parts = [value]
    for width in (64, 32, 16):
        first = lane_bit(shape, width)
        turned = [pltpu.roll(part, width, 1) for part in parts]
        parts = [
            side
            for part, turn in zip(parts, turned)
            for side in (jnp.where(first, part, turn), jnp.where(first, turn, part))
        ]
    return parts


def band_sums(parts, shape):
    for width in (1, 2, 4, 8):
        first = lane_bit(shape, width)
        merged = []
        for a, b in zip(parts[0::2], parts[1::2]):
            other = jnp.where(first, b, a)
            other = jnp.where(first, pltpu.roll(other, LANES - width, 1), pltpu.roll(other, width, 1))
            merged.append(jnp.where(first, a, b) + other)
        parts = merged
    return parts[0]


def band_copies(value, shape):
    parts = [value]
    for width in (8, 4, 2, 1):
        first = lane_bit(shape, width)
        parts = [
            side
            for part in parts
            for side in (
                jnp.where(first, part, pltpu.roll(part, width, 1)),
                jnp.where(first, pltpu.roll(part, LANES - width, 1), part),
            )
        ]
    return parts


def lines(ref, start):
    return jnp.concatenate([ref[pl.ds(row, PW, stride=BLK), :] for row in start], axis=0)


def source_masks():
    group = lax.broadcasted_iota(jnp.int32, (1, LANES), 1) // LB
    return [group == s for s in range(BD)]


def scatter_kernel(cells, recv, zh, zl, mh, ml, sent, dense, turned, fields, bh, bl):
    zero = jnp.zeros((256, LANES), f32)

    def clear(i, carry):
        dense[pl.ds(pl.multiple_of(i * 256, 256), 256), :] = zero
        return carry

    lax.fori_loop(0, SLAB // 256, clear, 0)

    def turn(i, carry):
        at = pl.multiple_of(i * LANES, LANES)
        turned[pl.ds(at, LANES), :] = recv[:, pl.ds(at, LANES)].T
        return carry

    lax.fori_loop(0, KW // LANES, turn, 0)
    masks = source_masks()

    def place(i, carry):
        for j in range(8):
            k = i * 8 + j
            row = turned[pl.ds(k, 1), :]
            for s in range(BD):
                cell = cells[s * KW + k]
                pltpu.store(dense.at[pl.ds(cell, 1), :], row, mask=masks[s])
        return carry

    lax.fori_loop(0, KW // 8, place, 0)
    table = (zh[...], zl[...])

    def along_z(i, carry):
        y, pair = i // 6, i % 6
        folded = []
        for side in range(2):
            base = (y * G + (pair * 2 + side) * 8) * G
            tiles = []
            for r in range(0, G, 8):
                parts = [dense[pl.ds(pl.multiple_of(base + xl * G + r, 8), 8), :] for xl in range(8)]
                tiles.append(gather_groups(parts, (8, LANES)))
            folded.append(jnp.concatenate(tiles, axis=0))
        out = dot3(table, split(jnp.concatenate(folded, axis=1)))
        at = pl.multiple_of(y * G, G)
        fields[pair * 2, pl.ds(at, G), :] = out[:, :LANES]
        fields[pair * 2 + 1, pl.ds(at, G), :] = out[:, LANES:]
        return carry

    lax.fori_loop(0, GY * 6, along_z, 0)

    def twelve(i, carry):
        at = pl.multiple_of(i * 16, 16)
        e = [fields[xh, pl.ds(at, 16), :] for xh in range(12)]
        c = cos12([e[0]] + [e[j] + e[12 - j] for j in range(1, 6)] + [e[6]])
        s = sin12([None] + [e[j] - e[12 - j] for j in range(1, 6)])
        for p in range(6):
            high, low = split(jnp.concatenate([c[p], c[6] if p == 0 else s[p]], axis=1))
            bh[p, pl.ds(at, 16), :] = high
            bl[p, pl.ds(at, 16), :] = low
        return carry

    lax.fori_loop(0, GY * G // 16, twelve, 0)

    def along_x(y, carry):
        at = pl.multiple_of(y * G, G)
        for p in range(6):
            data = (bh[p, pl.ds(at, G), :], bl[p, pl.ds(at, G), :])
            out = dot3(data, (mh[p], ml[p]))
            for side, m in enumerate((p, 6 if p == 0 else 12 - p)):
                for z in range(GY):
                    sent[pl.ds(y * COLS + z * 12 + m, PW, stride=BLK), :] = out[
                        z * PW : (z + 1) * PW, side * LANES : (side + 1) * LANES
                    ]
        return carry

    lax.fori_loop(0, GY, along_x, 0)


def density_kernel(recv, yh, yl, share, fields, sums):
    table = (yh[...], yl[...])

    def along_y(i, carry):
        data = [lines(recv, [y * COLS + i * 2 + side for y in range(GY)]) for side in range(2)]
        out = dot3(table, split(jnp.concatenate(data, axis=1)))
        for side in range(2):
            fields[pl.ds(pl.multiple_of((i * 2 + side) * G, G), G), :] = out[:, side * LANES : (side + 1) * LANES]
        return carry

    lax.fori_loop(0, COLS // 2, along_y, 0)
    weight = share[...]

    def squares(i, carry):
        parts = []
        for j in range(LB):
            value = fields[pl.ds(pl.multiple_of(j * SUM_ROWS + i * 8, 8), 8), :]
            parts.append(weight * value * value)
        sums[pl.ds(pl.multiple_of(i * 8, 8), 8), :] = band_sums(parts, (8, LANES))
        return carry

    lax.fori_loop(0, SUM_ROWS // 8, squares, 0)


def potential_kernel(density, external, fields, yh, yl, sent, product):
    def multiply(i, carry):
        at = pl.multiple_of(i * 8, 8)
        dens = density[pl.ds(at, 8), :]
        root = jnp.exp(jnp.log(dens) * (1.0 / 3.0))
        root = root - (root - dens / (root * root)) * (1.0 / 3.0)
        copies = band_copies(external[pl.ds(at, 8), :] - slater * root, (8, LANES))
        for j in range(LB):
            row = pl.ds(pl.multiple_of(j * SUM_ROWS + i * 8, 8), 8)
            product[row, :] = copies[j] * fields[row, :]
        return carry

    lax.fori_loop(0, SUM_ROWS // 8, multiply, 0)
    table = (yh[...], yl[...])

    def along_y(i, carry):
        data = [product[pl.ds(pl.multiple_of((i * 2 + side) * G, G), G), :] for side in range(2)]
        out = dot3(table, split(jnp.concatenate(data, axis=1)))
        for side in range(2):
            for y in range(GY):
                sent[pl.ds(y * COLS + i * 2 + side, PW, stride=BLK), :] = out[
                    y * PW : (y + 1) * PW, side * LANES : (side + 1) * LANES
                ]
        return carry

    lax.fori_loop(0, COLS // 2, along_y, 0)


def gather_kernel(cells, recv, zh, zl, mh, ml, terms, dense, turned, uv, bh, bl):
    table = (zh[...], zl[...])

    def plane(y, carry):
        for p in range(6):
            data = [
                lines(recv, [y * COLS + z * 12 + m for z in range(GY)]) for m in (p, 6 if p == 0 else 12 - p)
            ]
            out = dot3(split(jnp.concatenate(data, axis=1)), (mh[p], ml[p]))
            uv[p] = out

        def twelve(i, inner):
            at = pl.multiple_of(i * 16, 16)
            u = [uv[p, pl.ds(at, 16), :LANES] for p in range(6)] + [uv[0, pl.ds(at, 16), LANES:]]
            v = [None] + [uv[p, pl.ds(at, 16), LANES:] for p in range(1, 6)]
            c, s = cos12(u), sin12(v)
            x = [c[0]] + [c[j] + s[j] for j in range(1, 6)] + [c[6]] + [c[j] - s[j] for j in range(5, 0, -1)]
            for p in range(6):
                high, low = split(jnp.concatenate([x[2 * p], x[2 * p + 1]], axis=1))
                bh[p, pl.ds(at, 16), :] = high
                bl[p, pl.ds(at, 16), :] = low
            return inner

        lax.fori_loop(0, G // 16, twelve, 0)

        def along_z(pair, inner):
            out = dot3(table, (bh[pair], bl[pair]))
            for side in range(2):
                base = (y * G + (pair * 2 + side) * 8) * G
                for r in range(0, G, 8):
                    copies = spread_groups(out[r : r + 8, side * LANES : (side + 1) * LANES], (8, LANES))
                    for xl in range(8):
                        dense[pl.ds(pl.multiple_of(base + xl * G + r, 8), 8), :] = copies[xl]
            return inner

        lax.fori_loop(0, 6, along_z, 0)
        return carry

    lax.fori_loop(0, GY, plane, 0)
    masks = source_masks()

    def pick(i, carry):
        for j in range(8):
            k = i * 8 + j
            row = dense[pl.ds(cells[k], 1), :]
            for s in range(1, BD):
                row = jnp.where(masks[s], dense[pl.ds(cells[s * KW + k], 1), :], row)
            turned[pl.ds(k, 1), :] = row
        return carry

    lax.fori_loop(0, KW // 8, pick, 0)

    def turn(i, carry):
        at = pl.multiple_of(i * LANES, LANES)
        terms[:, pl.ds(at, LANES)] = turned[pl.ds(at, LANES), :].T
        return carry

    lax.fori_loop(0, KW // LANES, turn, 0)


def call(kernel, out_shapes, scratch, scalars, *operands):
    vmem = pl.BlockSpec(memory_space=pltpu.VMEM)
    smem = pl.BlockSpec(memory_space=pltpu.SMEM)
    return pl.pallas_call(
        kernel,
        out_shape=out_shapes,
        in_specs=[smem] * scalars + [vmem] * (len(operands) - scalars),
        out_specs=jax.tree.map(lambda _: vmem, out_shapes),
        scratch_shapes=scratch,
        compiler_params=pltpu.CompilerParams(vmem_limit_bytes=56 * 1024 * 1024),
    )(*operands)


def array(*shape):
    return jax.ShapeDtypeStruct(shape, f32)


def matmul(left_side, right_side):
    return jnp.dot(left_side, right_side, precision=highest, preferred_element_type=f32)


def loewdin(intersection):
    frob_norm = jnp.sqrt(jnp.sum(intersection * intersection))
    identity = jnp.eye(intersection.shape[0], dtype=f32)
    y_iter = intersection / frob_norm
    z_iter = identity
    for repeat in range(NS_ITERS):
        middle = 1.5 * identity - 0.5 * matmul(z_iter, y_iter)
        y_iter = matmul(y_iter, middle)
        z_iter = matmul(middle, z_iter)
    return z_iter / jnp.sqrt(frob_norm)


def total(values):
    axes = ("pw", "band")
    pieces = lax.all_to_all(values, axes, split_axis=0, concat_axis=0, tiled=True)
    row = jnp.sum(pieces, axis=0, keepdims=True)
    copies = jnp.broadcast_to(row, values.shape)
    return lax.all_to_all(copies, axes, split_axis=0, concat_axis=0, tiled=True)


def band_total(values):
    values = values + lax.ppermute(values, "band", [(i, i ^ 1) for i in range(BD)])
    others = [lax.ppermute(values, "band", [(i, (i + 2 * step) % BD) for i in range(BD)]) for step in (1, 2, 3)]
    return values + ((others[0] + others[2]) + others[1])


def to_sums(planes):
    values = planes.reshape(GY, G, BD, 12).transpose(0, 3, 1, 2).reshape(LB, SUM_ROWS, BD)
    return values.transpose(1, 2, 0).reshape(SUM_ROWS, LANES)


def from_sums(sums):
    values = sums.reshape(SUM_ROWS, BD, LB).transpose(2, 0, 1).reshape(GY, 12, G, BD)
    return values.transpose(0, 2, 3, 1).reshape(GY, G * G)


def shards(coefficients, occupancy, kinetic, cell_map, potential_ext, core_density):
    table = tables()
    pw_pos = lax.axis_index("pw")
    band_pos = lax.axis_index("band")
    cells = cell_map - pw_pos * SLAB
    share = lax.dynamic_slice_in_dim(occupancy / NB, band_pos * LB, LB)
    share = jnp.tile(share, BD).reshape(1, LANES)
    core = to_sums(core_density)
    external = to_sums(potential_ext)

    intersection = total(matmul(coefficients, coefficients.T)) / NPW
    weights, pullback = jax.vjp(loewdin, intersection)
    rotated = matmul(weights.T, coefficients)
    block = lax.all_to_all(rotated, "band", split_axis=0, concat_axis=0, tiled=True)
    sent = call(
        scatter_kernel,
        array(ROWS, LANES),
        [
            pltpu.VMEM((SLAB, LANES), f32),
            pltpu.VMEM((KW, LANES), f32),
            pltpu.VMEM((12, GY * G, LANES), f32),
            pltpu.VMEM((6, GY * G, 2 * LANES), bf16),
            pltpu.VMEM((6, GY * G, 2 * LANES), bf16),
        ],
        1,
        cells,
        block,
        *table["z_out"],
        *table["mix"],
    )
    received = lax.all_to_all(sent, "pw", split_axis=0, concat_axis=0, tiled=True)
    fields, sums = call(
        density_kernel,
        (array(ROWS, LANES), array(SUM_ROWS, LANES)),
        [],
        0,
        received,
        *table["y_out"],
        share,
    )
    density = core + band_total(sums)
    sent = call(
        potential_kernel,
        array(ROWS, LANES),
        [pltpu.VMEM((ROWS, LANES), f32)],
        0,
        density,
        external,
        fields,
        *table["y_in"],
    )
    received = lax.all_to_all(sent, "pw", split_axis=0, concat_axis=0, tiled=True)
    terms = call(
        gather_kernel,
        array(NB, KW),
        [
            pltpu.VMEM((SLAB, LANES), f32),
            pltpu.VMEM((KW, LANES), f32),
            pltpu.VMEM((6, G, 2 * LANES), f32),
            pltpu.VMEM((6, G, 2 * LANES), bf16),
            pltpu.VMEM((6, G, 2 * LANES), bf16),
        ],
        1,
        cells,
        received,
        *table["z_in"],
        *table["mix_t"],
    )
    row_term = lax.all_to_all(terms, "band", split_axis=0, concat_axis=0, tiled=True)
    grad_rotated = occupancy[:, None] * (kinetic[None, :] * rotated + row_term)
    grad_weights = total(matmul(coefficients, grad_rotated.T))
    (grad_intersection,) = pullback(grad_weights)
    grad_coef = (
        matmul(weights, grad_rotated) + matmul(grad_intersection + grad_intersection.T, coefficients) / NPW
    )
    return (grad_coef, from_sums(density))


def solution(mesh):
    placed = (
        P(None, ("pw", "band")),
        P(),
        P(("pw", "band")),
        P("pw"),
        P("pw", None),
        P("pw", None),
    )
    return jax.shard_map(
        shards,
        mesh=mesh,
        in_specs=placed,
        out_specs=(P(None, ("pw", "band")), P("pw", None)),
        check_vma=False,
    )
```

```python
import functools
import math

import jax
import jax.numpy as jnp
import ml_dtypes
import numpy as np
from jax import lax
from jax.experimental import pallas as pl
from jax.experimental.pallas import tpu as pltpu
from jax.sharding import PartitionSpec as P

G = 96
NPW = 393216
NB = 128
NS_ITERS = 4
PW = 16
BD = 8
LB = NB // BD
GY = G // PW
PARTS = 2
BLOCKS = ((0, 6), (1, 11), (2, 10), (3, 9), (4, 8), (5, 7))
PAIRS = len(BLOCKS) // PARTS
XB = 2 * PAIRS
COLS = GY * XB
HALF = G // 2
WIDE = XB * 128
SLAB = GY * G * G
KW = NPW // (PW * BD)
BLK = GY * COLS
ROWS = PW * BLK
SUM_ROWS = GY * HALF
LANES = 128

highest = lax.Precision.HIGHEST
slater = 0.9847450218426965
bf16 = jnp.bfloat16
f32 = jnp.float32


def halves(table):
    high = table.astype(ml_dtypes.bfloat16)
    low = (table - high.astype(np.float64)).astype(ml_dtypes.bfloat16)
    return high, low


def tables():
    counter = np.arange(G)
    phases = 2.0 * np.pi / G * (counter[:, None] * counter[None, :] % G)
    cas = np.cos(phases) + np.sin(phases)
    order = (np.arange(PW)[None, :] * GY + np.arange(GY)[:, None]).reshape(-1)
    scaled = cas / math.sqrt(NPW)
    mixes = []
    small = np.arange(8)

    def mix(m):
        beta = 2.0 * np.pi / G * (small[:, None] * (m + 12 * small[None, :]))
        even = np.kron(np.cos(beta) + np.sin(beta), np.eye(LB))
        odd = np.kron(np.cos(beta) - np.sin(beta), np.eye(LB))
        return even, odd

    zero = np.zeros((LANES, LANES))
    mixes.append(np.block([[mix(0)[0], zero], [zero, mix(6)[0]]]))
    for m in range(1, 6):
        here, there = mix(m), mix(12 - m)
        mixes.append(np.block([[here[0], there[0]], [here[1], -there[1]]]))
    mixes = np.stack(mixes)
    return dict(
        z_out=halves(scaled[order, :]),
        y_out=halves(cas[:, order]),
        y_in=halves(cas[order, :]),
        z_in=halves(scaled[:, order]),
        mix=halves(mixes),
        mix_t=halves(np.swapaxes(mixes, 1, 2)),
    )


ROOT3 = math.sqrt(3.0) / 2.0


def cos12(e):
    a0, a1, a2 = e[0] + e[6], e[1] + e[5], e[2] + e[4]
    b0, b1, b2 = e[0] - e[6], e[1] - e[5], e[2] - e[4]
    t = ROOT3 * b1
    h = b0 + 0.5 * b2
    r = 0.5 * (a1 + a2)
    d = 0.5 * (a1 - a2)
    return [
        a0 + a1 + a2 + e[3],
        h + t,
        a0 + d - e[3],
        b0 - b2,
        a0 - r + e[3],
        h - t,
        a0 - a1 + a2 - e[3],
    ]


def sin12(o):
    p1, p2 = o[1] + o[5], o[2] + o[4]
    r1, r2 = o[1] - o[5], o[2] - o[4]
    h = 0.5 * p1 + o[3]
    t = ROOT3 * p2
    return [None, h + t, ROOT3 * (r1 + r2), p1 - o[3], ROOT3 * (r1 - r2), h - t]


def split(values):
    high = values.astype(bf16)
    return high, (values - high.astype(f32)).astype(bf16)


def dot(a, b):
    return jnp.dot(a, b, preferred_element_type=f32)


def dot3(a, b):
    return dot(a[0], b[0]) + (dot(a[0], b[1]) + dot(a[1], b[0]))


def lane_bit(shape, bit):
    return (lax.broadcasted_iota(jnp.int32, shape, 1) & bit) == 0


def gather_groups(parts, shape):
    for width in (16, 32, 64):
        first = lane_bit(shape, width)
        parts = [
            jnp.where(first, a, b) + pltpu.roll(jnp.where(first, b, a), width, 1)
            for a, b in zip(parts[0::2], parts[1::2])
        ]
    return parts[0]


def spread_groups(value, shape):
    parts = [value]
    for width in (64, 32, 16):
        first = lane_bit(shape, width)
        turned = [pltpu.roll(part, width, 1) for part in parts]
        parts = [
            side
            for part, turn in zip(parts, turned)
            for side in (jnp.where(first, part, turn), jnp.where(first, turn, part))
        ]
    return parts


def lines(ref, start):
    return jnp.concatenate([ref[pl.ds(row, PW, stride=BLK), :] for row in start], axis=0)


def source_masks():
    group = lax.broadcasted_iota(jnp.int32, (1, LANES), 1) // LB
    return [group == s for s in range(BD)]


def scatter_kernel(cells, recv, zh, zl, mh, ml, sent0, sent1, dense, turned, fields, bh, bl):
    zero = jnp.zeros((256, LANES), f32)

    def clear(i, carry):
        dense[pl.ds(pl.multiple_of(i * 256, 256), 256), :] = zero
        return carry

    lax.fori_loop(0, SLAB // 256, clear, 0)

    def turn(i, carry):
        at = pl.multiple_of(i * LANES, LANES)
        turned[pl.ds(at, LANES), :] = recv[:, pl.ds(at, LANES)].T
        return carry

    lax.fori_loop(0, KW // LANES, turn, 0)
    masks = source_masks()

    def place(i, carry):
        for j in range(8):
            k = i * 8 + j
            row = turned[pl.ds(k, 1), :]
            for s in range(BD):
                cell = cells[s * KW + k]
                pltpu.store(dense.at[pl.ds(cell, 1), :], row, mask=masks[s])
        return carry

    lax.fori_loop(0, KW // 8, place, 0)
    table = (zh[...], zl[...])

    def along_z(i, carry):
        y, quad = i // 3, i % 3
        folded = []
        for side in range(4):
            base = (y * G + (quad * 4 + side) * 8) * G
            tiles = []
            for r in range(0, G, 8):
                parts = [dense[pl.ds(pl.multiple_of(base + xl * G + r, 8), 8), :] for xl in range(8)]
                tiles.append(gather_groups(parts, (8, LANES)))
            folded.append(jnp.concatenate(tiles, axis=0))
        out = dot3(table, split(jnp.concatenate(folded, axis=1)))
        at = pl.multiple_of(y * G, G)
        for side in range(4):
            fields[quad * 4 + side, pl.ds(at, G), :] = out[:, side * LANES : (side + 1) * LANES]
        return carry

    lax.fori_loop(0, GY * 3, along_z, 0)

    def twelve(i, carry):
        at = pl.multiple_of(i * 16, 16)
        e = [fields[xh, pl.ds(at, 16), :] for xh in range(12)]
        c = cos12([e[0]] + [e[j] + e[12 - j] for j in range(1, 6)] + [e[6]])
        s = sin12([None] + [e[j] - e[12 - j] for j in range(1, 6)])
        for p in range(6):
            high, low = split(jnp.concatenate([c[p], c[6] if p == 0 else s[p]], axis=1))
            bh[p, pl.ds(at, 16), :] = high
            bl[p, pl.ds(at, 16), :] = low
        return carry

    lax.fori_loop(0, GY * G // 16, twelve, 0)

    sent = (sent0, sent1)

    def along_x(y, carry):
        at = pl.multiple_of(y * G, G)
        for p in range(6):
            data = (bh[p, pl.ds(at, G), :], bl[p, pl.ds(at, G), :])
            out = dot3(data, (mh[p], ml[p]))
            for side in range(2):
                for z in range(GY):
                    row = y * COLS + z * XB + p % PAIRS * 2 + side
                    sent[p // PAIRS][pl.ds(row, PW, stride=BLK), :] = out[
                        z * PW : (z + 1) * PW, side * LANES : (side + 1) * LANES
                    ]
        return carry

    lax.fori_loop(0, GY, along_x, 0)


def density_kernel(recv, yh, yl, pack0, pack1, share, *rest):
    fields, sums = rest[-2:]
    table = (yh[...], yl[...])
    weight = share[...]

    def along_y(z, carry):
        data = [lines(recv, [y * COLS + z * XB + i for y in range(GY)]) for i in range(XB)]
        out = dot3(table, split(jnp.concatenate(data, axis=1)))
        for i in range(XB):
            at = pl.multiple_of((z * XB + i) * G, G)
            fields[pl.ds(at, G), :] = out[:, i * LANES : (i + 1) * LANES]
        high, low = split(weight * out * out)
        first, second = pack0[...], pack1[...]
        added = dot(high[:HALF], first) + dot(low[:HALF], first)
        added = added + (dot(high[HALF:], second) + dot(low[HALF:], second))
        sums[pl.ds(pl.multiple_of(z * HALF, HALF), HALF), :] = added
        return carry

    lax.fori_loop(0, GY, along_y, 0)


def potential_kernel(density, external, fields, yh, yl, open0, open1, sent):
    table = (yh[...], yl[...])

    def along_y(z, carry):
        at = pl.multiple_of(z * HALF, HALF)
        dens = density[pl.ds(at, HALF), :]
        root = jnp.exp(jnp.log(dens) * (1.0 / 3.0))
        root = root - (root - dens / (root * root)) * (1.0 / 3.0)
        high, low = split(external[pl.ds(at, HALF), :] - slater * root)
        first, second = open0[...], open1[...]
        spread = [dot(high, first) + dot(low, first), dot(high, second) + dot(low, second)]
        value = [fields[pl.ds(pl.multiple_of((z * XB + i) * G, G), G), :] for i in range(XB)]
        product = jnp.concatenate(spread, axis=0) * jnp.concatenate(value, axis=1)
        out = dot3(table, split(product))
        for i in range(XB):
            for y in range(GY):
                sent[pl.ds(y * COLS + z * XB + i, PW, stride=BLK), :] = out[
                    y * PW : (y + 1) * PW, i * LANES : (i + 1) * LANES
                ]
        return carry

    lax.fori_loop(0, GY, along_y, 0)


def gather_kernel(cells, recv0, recv1, zh, zl, mh, ml, terms, dense, turned, uv, bh, bl):
    table = (zh[...], zl[...])
    recv = (recv0, recv1)

    def along_x(y, carry):
        at = pl.multiple_of(y * G, G)
        for p in range(6):
            first = p % PAIRS * 2
            data = [
                lines(recv[p // PAIRS], [y * COLS + z * XB + first + side for z in range(GY)]) for side in range(2)
            ]
            uv[p, pl.ds(at, G), :] = dot3(split(jnp.concatenate(data, axis=1)), (mh[p], ml[p]))
        return carry

    lax.fori_loop(0, GY, along_x, 0)

    def twelve(i, carry):
        at = pl.multiple_of(i * 16, 16)
        u = [uv[p, pl.ds(at, 16), :LANES] for p in range(6)] + [uv[0, pl.ds(at, 16), LANES:]]
        v = [None] + [uv[p, pl.ds(at, 16), LANES:] for p in range(1, 6)]
        c, s = cos12(u), sin12(v)
        x = [c[0]] + [c[j] + s[j] for j in range(1, 6)] + [c[6]] + [c[j] - s[j] for j in range(5, 0, -1)]
        for quad in range(3):
            high, low = split(jnp.concatenate(x[4 * quad : 4 * quad + 4], axis=1))
            bh[quad, pl.ds(at, 16), :] = high
            bl[quad, pl.ds(at, 16), :] = low
        return carry

    lax.fori_loop(0, GY * G // 16, twelve, 0)

    def along_z(i, carry):
        y, quad = i // 3, i % 3
        at = pl.multiple_of(y * G, G)
        out = dot3(table, (bh[quad, pl.ds(at, G), :], bl[quad, pl.ds(at, G), :]))
        for side in range(4):
            base = (y * G + (quad * 4 + side) * 8) * G
            for r in range(0, G, 8):
                copies = spread_groups(out[r : r + 8, side * LANES : (side + 1) * LANES], (8, LANES))
                for xl in range(8):
                    dense[pl.ds(pl.multiple_of(base + xl * G + r, 8), 8), :] = copies[xl]
        return carry

    lax.fori_loop(0, GY * 3, along_z, 0)
    masks = source_masks()

    def pick(i, carry):
        for j in range(8):
            k = i * 8 + j
            row = dense[pl.ds(cells[k], 1), :]
            for s in range(1, BD):
                row = jnp.where(masks[s], dense[pl.ds(cells[s * KW + k], 1), :], row)
            turned[pl.ds(k, 1), :] = row
        return carry

    lax.fori_loop(0, KW // 8, pick, 0)

    def turn(i, carry):
        at = pl.multiple_of(i * LANES, LANES)
        terms[:, pl.ds(at, LANES)] = turned[pl.ds(at, LANES), :].T
        return carry

    lax.fori_loop(0, KW // LANES, turn, 0)


def pullback_kernel(grads, s, y0, y1, y2, y3, z1, z2, z3, z4, t1, t2, t3, t4, out):
    def mul(a, b):
        return jnp.dot(a[...], b[...], precision=highest, preferred_element_type=f32)

    y, z, t = (y0, y1, y2, y3), (None, z1, z2, z3, z4), (None, t1, t2, t3, t4)
    values = s[...]
    squared = jnp.sum(values * values, keepdims=True)
    frob = jnp.sqrt(squared)
    root = jnp.sqrt(frob)
    given = grads[...]
    zb = given / root
    fb = -0.5 * jnp.sum(given * z4[...], keepdims=True) / (frob * root)
    yb = None
    for k in range(NS_ITERS, 0, -1):
        tb = zb if k == 1 else mul(zb, z[k - 1])
        if yb is not None:
            tb = tb + mul(y[k - 1], yb)
        before = tb if k == 1 else mul(z[k - 1], tb)
        before = -0.5 * before
        if yb is not None:
            before = before + mul(yb, t[k])
        if k > 1:
            zb = mul(t[k], zb) - 0.5 * mul(tb, y[k - 1])
        yb = before
    fb = fb - jnp.sum(yb * values, keepdims=True) / squared
    grad = yb / frob + fb * (values / frob)
    out[...] = (grad + grad.T) / NPW


def call(kernel, out_shapes, scratch, scalars, *operands, unread=()):
    vmem = pl.BlockSpec(memory_space=pltpu.VMEM)
    smem = pl.BlockSpec(memory_space=pltpu.SMEM)
    return pl.pallas_call(
        kernel,
        out_shape=out_shapes,
        in_specs=[smem] * scalars
        + [vmem] * (len(operands) - scalars)
        + [pl.BlockSpec(memory_space=pl.ANY)] * len(unread),
        out_specs=jax.tree.map(lambda _: vmem, out_shapes),
        scratch_shapes=scratch,
        compiler_params=pltpu.CompilerParams(vmem_limit_bytes=58 * 1024 * 1024),
    )(*operands, *unread)


def array(*shape):
    return jax.ShapeDtypeStruct(shape, f32)


def matmul(left_side, right_side):
    return jnp.dot(left_side, right_side, precision=highest, preferred_element_type=f32)


def loewdin(intersection):
    frob_norm = jnp.sqrt(jnp.sum(intersection * intersection))
    identity = jnp.eye(intersection.shape[0], dtype=f32)
    ys, zs, ts = [intersection / frob_norm], [], []
    for repeat in range(NS_ITERS):
        product = matmul(zs[-1], ys[-1]) if zs else ys[-1]
        ts.append(1.5 * identity - 0.5 * product)
        zs.append(matmul(ts[-1], zs[-1]) if zs else ts[-1])
        if repeat < NS_ITERS - 1:
            ys.append(matmul(ys[-1], ts[-1]))
    return zs[-1] / jnp.sqrt(frob_norm), (*ys, *zs, *ts)


def total(values):
    axes = ("pw", "band")
    pieces = lax.all_to_all(values, axes, split_axis=0, concat_axis=0, tiled=True)
    row = jnp.sum(pieces, axis=0, keepdims=True)
    copies = jnp.broadcast_to(row, values.shape)
    return lax.all_to_all(copies, axes, split_axis=0, concat_axis=0, tiled=True)


def band_total(values):
    values = values + lax.ppermute(values, "band", [(i, i ^ 1) for i in range(BD)])
    others = [lax.ppermute(values, "band", [(i, (i + 2 * step) % BD) for i in range(BD)]) for step in (1, 2, 3)]
    return values + ((others[0] + others[2]) + others[1])


def packings():
    chosen = np.zeros((PARTS, 2, G, LANES))
    packed = np.zeros((PARTS, 2, WIDE, LANES))
    for part in range(PARTS):
        blocks = [m for pair in BLOCKS[part * PAIRS : (part + 1) * PAIRS] for m in pair]
        for half in range(2):
            for i, m in enumerate(blocks):
                for q in range(BD):
                    lane = half * 64 + i * BD + q
                    chosen[part, half, m + 12 * q, lane] = 1
                    row = i * LANES + q * LB
                    packed[part, half, row : row + LB, lane] = 1
    return chosen, packed


def to_sums(planes, chosen):
    values = planes.reshape(GY, 2, HALF, G)
    packed = matmul(values[:, 0], chosen[0]) + matmul(values[:, 1], chosen[1])
    return packed.reshape(SUM_ROWS, LANES)


def from_sums(parts, chosen):
    halves_of_y = [
        sum(matmul(parts[part], chosen[part, half].T) for part in range(PARTS)).reshape(GY, 1, HALF, G)
        for half in range(2)
    ]
    return jnp.concatenate(halves_of_y, axis=1).reshape(GY, G * G)


def shards(coefficients, occupancy, kinetic, cell_map, potential_ext, core_density):
    table = tables()
    chosen, packed = packings()
    chosen = chosen.astype(np.float32)
    pack = packed[0].astype(ml_dtypes.bfloat16)
    unpack = np.swapaxes(pack, 1, 2)
    unused = (1.0 - chosen.sum(axis=(1, 2))).astype(np.float32)
    pw_pos = lax.axis_index("pw")
    band_pos = lax.axis_index("band")
    cells = cell_map - pw_pos * SLAB
    share = lax.dynamic_slice_in_dim(occupancy / NB, band_pos * LB, LB)
    share = jnp.tile(share, XB * BD).reshape(1, WIDE)
    core = [to_sums(core_density, chosen[part]) + unused[part] for part in range(PARTS)]
    external = [to_sums(potential_ext, chosen[part]) for part in range(PARTS)]

    intersection = total(matmul(coefficients, coefficients.T)) / NPW
    weights, iterates = loewdin(intersection)
    rotated = matmul(weights.T, coefficients)
    block = lax.all_to_all(rotated, "band", split_axis=0, concat_axis=0, tiled=True)
    sent = call(
        scatter_kernel,
        [array(ROWS, LANES)] * PARTS,
        [
            pltpu.VMEM((SLAB, LANES), f32),
            pltpu.VMEM((KW, LANES), f32),
            pltpu.VMEM((12, GY * G, LANES), f32),
            pltpu.VMEM((6, GY * G, 2 * LANES), bf16),
            pltpu.VMEM((6, GY * G, 2 * LANES), bf16),
        ],
        1,
        cells,
        block,
        *table["z_out"],
        *table["mix"],
    )
    exchange = functools.partial(lax.all_to_all, axis_name="pw", split_axis=0, concat_axis=0, tiled=True)
    density, returned, after = [], [], []
    for part in range(PARTS):
        received = exchange(sent[part])
        fields, sums = call(
            density_kernel,
            (array(ROWS, LANES), array(SUM_ROWS, LANES)),
            [],
            0,
            received,
            *table["y_out"],
            *pack,
            share,
            unread=after,
        )
        density.append(core[part] + band_total(sums))
        product = call(
            potential_kernel,
            array(ROWS, LANES),
            [],
            0,
            density[part],
            external[part],
            fields,
            *table["y_in"],
            *unpack,
        )
        after = [product]
        returned.append(exchange(product))
    terms = call(
        gather_kernel,
        array(NB, KW),
        [
            pltpu.VMEM((SLAB, LANES), f32),
            pltpu.VMEM((KW, LANES), f32),
            pltpu.VMEM((6, GY * G, 2 * LANES), f32),
            pltpu.VMEM((3, GY * G, 4 * LANES), bf16),
            pltpu.VMEM((3, GY * G, 4 * LANES), bf16),
        ],
        1,
        cells,
        *returned,
        *table["z_in"],
        *table["mix_t"],
    )
    row_term = lax.all_to_all(terms, "band", split_axis=0, concat_axis=0, tiled=True)
    grad_rotated = occupancy[:, None] * (kinetic[None, :] * rotated + row_term)
    grad_weights = total(matmul(coefficients, grad_rotated.T))
    grad_intersection = call(pullback_kernel, array(NB, NB), [], 0, grad_weights, intersection, *iterates)
    grad_coef = matmul(weights, grad_rotated) + matmul(grad_intersection, coefficients)
    return (grad_coef, from_sums(density, chosen))


def solution(mesh):
    placed = (
        P(None, ("pw", "band")),
        P(),
        P(("pw", "band")),
        P("pw"),
        P("pw", None),
        P("pw", None),
    )
    return jax.shard_map(
        shards,
        mesh=mesh,
        in_specs=placed,
        out_specs=(P(None, ("pw", "band")), P("pw", None)),
        check_vma=False,
    )
```

```python
import functools
import math

import jax
import jax.numpy as jnp
import ml_dtypes
import numpy as np
from jax import lax
from jax.experimental import pallas as pl
from jax.experimental.pallas import tpu as pltpu
from jax.sharding import PartitionSpec as P

G = 96
NPW = 393216
NB = 128
NS_ITERS = 4
PW = 16
BD = 8
LB = NB // BD
GY = G // PW
PARTS = 2
BLOCKS = ((0, 6), (1, 11), (2, 10), (3, 9), (4, 8), (5, 7))
PAIRS = len(BLOCKS) // PARTS
XB = 2 * PAIRS
COLS = GY * XB
HALF = G // 2
WIDE = XB * 128
SLAB = GY * G * G
KW = NPW // (PW * BD)
BLK = GY * COLS
ROWS = PW * BLK
SUM_ROWS = GY * HALF
LANES = 128

highest = lax.Precision.HIGHEST
slater = 0.9847450218426965
bf16 = jnp.bfloat16
f32 = jnp.float32


def halves(table):
    high = table.astype(ml_dtypes.bfloat16)
    low = (table - high.astype(np.float64)).astype(ml_dtypes.bfloat16)
    return high, low


def tables():
    counter = np.arange(G)
    phases = 2.0 * np.pi / G * (counter[:, None] * counter[None, :] % G)
    cas = np.cos(phases) + np.sin(phases)
    order = (np.arange(PW)[None, :] * GY + np.arange(GY)[:, None]).reshape(-1)
    scaled = cas / math.sqrt(NPW)
    mixes = []
    small = np.arange(8)

    def mix(m):
        beta = 2.0 * np.pi / G * (small[:, None] * (m + 12 * small[None, :]))
        even = np.kron(np.cos(beta) + np.sin(beta), np.eye(LB))
        odd = np.kron(np.cos(beta) - np.sin(beta), np.eye(LB))
        return even, odd

    zero = np.zeros((LANES, LANES))
    mixes.append(np.block([[mix(0)[0], zero], [zero, mix(6)[0]]]))
    for m in range(1, 6):
        here, there = mix(m), mix(12 - m)
        mixes.append(np.block([[here[0], there[0]], [here[1], -there[1]]]))
    mixes = np.stack(mixes)
    return dict(
        z_out=np.concatenate(halves(scaled[order, :])),
        y_out=np.concatenate(halves(cas[:, order])),
        y_in=np.concatenate(halves(cas[order, :])),
        z_in=np.concatenate(halves(scaled[:, order])),
        mix=halves(mixes),
        mix_t=halves(np.swapaxes(mixes, 1, 2)),
    )


ROOT3 = math.sqrt(3.0) / 2.0


def cos12(e):
    a0, a1, a2 = e[0] + e[6], e[1] + e[5], e[2] + e[4]
    b0, b1, b2 = e[0] - e[6], e[1] - e[5], e[2] - e[4]
    t = ROOT3 * b1
    h = b0 + 0.5 * b2
    r = 0.5 * (a1 + a2)
    d = 0.5 * (a1 - a2)
    return [
        a0 + a1 + a2 + e[3],
        h + t,
        a0 + d - e[3],
        b0 - b2,
        a0 - r + e[3],
        h - t,
        a0 - a1 + a2 - e[3],
    ]


def sin12(o):
    p1, p2 = o[1] + o[5], o[2] + o[4]
    r1, r2 = o[1] - o[5], o[2] - o[4]
    h = 0.5 * p1 + o[3]
    t = ROOT3 * p2
    return [None, h + t, ROOT3 * (r1 + r2), p1 - o[3], ROOT3 * (r1 - r2), h - t]


def split(values):
    high = values.astype(bf16)
    return high, (values - high.astype(f32)).astype(bf16)


def dot(a, b):
    return jnp.dot(a, b, preferred_element_type=f32)


def dot3(a, b):
    return dot(a[0], b[0]) + (dot(a[0], b[1]) + dot(a[1], b[0]))


def transform(table, b):
    rows = table.shape[0] // 2
    both = dot(table, b[0])
    return both[:rows] + (dot(table[:rows], b[1]) + both[rows:])


def lane_bit(shape, bit):
    return (lax.broadcasted_iota(jnp.int32, shape, 1) & bit) == 0


def gather_groups(parts, shape):
    for width in (16, 32, 64):
        first = lane_bit(shape, width)
        parts = [
            jnp.where(first, a, b) + pltpu.roll(jnp.where(first, b, a), width, 1)
            for a, b in zip(parts[0::2], parts[1::2])
        ]
    return parts[0]


def spread_groups(value, shape):
    parts = [value]
    for width in (64, 32, 16):
        first = lane_bit(shape, width)
        turned = [pltpu.roll(part, width, 1) for part in parts]
        parts = [
            side
            for part, turn in zip(parts, turned)
            for side in (jnp.where(first, part, turn), jnp.where(first, turn, part))
        ]
    return parts


def lines(ref, start):
    return jnp.concatenate([ref[pl.ds(row, PW, stride=BLK), :] for row in start], axis=0)


def source_masks():
    group = lax.broadcasted_iota(jnp.int32, (1, LANES), 1) // LB
    return [group == s for s in range(BD)]


def scatter_kernel(cells, recv, zt, mh, ml, *rest):
    sent, (dense, turned, fields, bh, bl) = rest[-7:-5], rest[-5:]
    zero = jnp.zeros((256, LANES), f32)

    def clear(i, carry):
        dense[pl.ds(pl.multiple_of(i * 256, 256), 256), :] = zero
        return carry

    lax.fori_loop(0, SLAB // 256, clear, 0)

    def turn(i, carry):
        at = pl.multiple_of(i * LANES, LANES)
        turned[pl.ds(at, LANES), :] = recv[:, pl.ds(at, LANES)].T
        return carry

    lax.fori_loop(0, KW // LANES, turn, 0)
    masks = source_masks()

    def place(i, carry):
        for j in range(16):
            k = i * 16 + j
            row = turned[pl.ds(k, 1), :]
            for s in range(BD):
                cell = cells[s * KW + k]
                pltpu.store(dense.at[pl.ds(cell, 1), :], row, mask=masks[s])
        return carry

    lax.fori_loop(0, KW // 16, place, 0)
    table = zt[...]

    def along_z(i, carry):
        y, quad = i // 3, i % 3
        folded = []
        for side in range(4):
            base = (y * G + (quad * 4 + side) * 8) * G
            tiles = []
            for r in range(0, G, 8):
                parts = [dense[pl.ds(pl.multiple_of(base + xl * G + r, 8), 8), :] for xl in range(8)]
                tiles.append(gather_groups(parts, (8, LANES)))
            folded.append(jnp.concatenate(tiles, axis=0))
        out = transform(table, split(jnp.concatenate(folded, axis=1)))
        at = pl.multiple_of(y * G, G)
        for side in range(4):
            fields[quad * 4 + side, pl.ds(at, G), :] = out[:, side * LANES : (side + 1) * LANES]
        return carry

    lax.fori_loop(0, GY * 3, along_z, 0)

    def twelve(i, carry):
        at = pl.multiple_of(i * 16, 16)
        e = [fields[xh, pl.ds(at, 16), :] for xh in range(12)]
        c = cos12([e[0]] + [e[j] + e[12 - j] for j in range(1, 6)] + [e[6]])
        s = sin12([None] + [e[j] - e[12 - j] for j in range(1, 6)])
        for p in range(6):
            high, low = split(jnp.concatenate([c[p], c[6] if p == 0 else s[p]], axis=1))
            bh[p, pl.ds(at, 16), :] = high
            bl[p, pl.ds(at, 16), :] = low
        return carry

    lax.fori_loop(0, GY * G // 16, twelve, 0)

    for p in range(6):
        out = dot3((bh[p], bl[p]), (mh[p], ml[p]))
        for side in range(2):
            for y in range(GY):
                for z in range(GY):
                    row = y * COLS + z * XB + p % PAIRS * 2 + side
                    at = y * G + z * PW
                    sent[p // PAIRS][pl.ds(row, PW, stride=BLK), :] = out[
                        at : at + PW, side * LANES : (side + 1) * LANES
                    ]


def density_kernel(recv, yt, pack0, pack1, share, *rest):
    fields, sums = rest[-2:]
    table = yt[...]
    weight = share[...]

    def along_y(z, carry):
        data = [lines(recv, [y * COLS + z * XB + i for y in range(GY)]) for i in range(XB)]
        out = transform(table, split(jnp.concatenate(data, axis=1)))
        for i in range(XB):
            at = pl.multiple_of((z * XB + i) * G, G)
            fields[pl.ds(at, G), :] = out[:, i * LANES : (i + 1) * LANES]
        high, low = split(weight * out * out)
        first, second = pack0[...], pack1[...]
        added = dot(high[:HALF], first) + dot(low[:HALF], first)
        added = added + (dot(high[HALF:], second) + dot(low[HALF:], second))
        sums[pl.ds(pl.multiple_of(z * HALF, HALF), HALF), :] = added
        return carry

    lax.fori_loop(0, GY, along_y, 0)


def potential_kernel(density, external, fields, yt, open0, open1, sent):
    table = yt[...]

    def along_y(z, carry):
        at = pl.multiple_of(z * HALF, HALF)
        dens = density[pl.ds(at, HALF), :]
        root = jnp.exp(jnp.log(dens) * (1.0 / 3.0))
        root = root - (root - dens / (root * root)) * (1.0 / 3.0)
        high, low = split(external[pl.ds(at, HALF), :] - slater * root)
        first, second = open0[...], open1[...]
        spread = [dot(high, first) + dot(low, first), dot(high, second) + dot(low, second)]
        value = [fields[pl.ds(pl.multiple_of((z * XB + i) * G, G), G), :] for i in range(XB)]
        product = jnp.concatenate(spread, axis=0) * jnp.concatenate(value, axis=1)
        out = transform(table, split(product))
        for i in range(XB):
            for y in range(GY):
                sent[pl.ds(y * COLS + z * XB + i, PW, stride=BLK), :] = out[
                    y * PW : (y + 1) * PW, i * LANES : (i + 1) * LANES
                ]
        return carry

    lax.fori_loop(0, GY, along_y, 0)


def gather_kernel(cells, recv0, recv1, zt, mh, ml, terms, dense, turned, uv, bh, bl):
    table = zt[...]
    recv = (recv0, recv1)
    for p in range(6):
        first = p % PAIRS * 2
        starts = [y * COLS + z * XB + first for y in range(GY) for z in range(GY)]
        data = [lines(recv[p // PAIRS], [row + side for row in starts]) for side in range(2)]
        uv[p] = dot3(split(jnp.concatenate(data, axis=1)), (mh[p], ml[p]))

    def twelve(i, carry):
        at = pl.multiple_of(i * 16, 16)
        u = [uv[p, pl.ds(at, 16), :LANES] for p in range(6)] + [uv[0, pl.ds(at, 16), LANES:]]
        v = [None] + [uv[p, pl.ds(at, 16), LANES:] for p in range(1, 6)]
        c, s = cos12(u), sin12(v)
        x = [c[0]] + [c[j] + s[j] for j in range(1, 6)] + [c[6]] + [c[j] - s[j] for j in range(5, 0, -1)]
        for quad in range(3):
            high, low = split(jnp.concatenate(x[4 * quad : 4 * quad + 4], axis=1))
            bh[quad, pl.ds(at, 16), :] = high
            bl[quad, pl.ds(at, 16), :] = low
        return carry

    lax.fori_loop(0, GY * G // 16, twelve, 0)

    def along_z(i, carry):
        y, quad = i // 3, i % 3
        at = pl.multiple_of(y * G, G)
        out = transform(table, (bh[quad, pl.ds(at, G), :], bl[quad, pl.ds(at, G), :]))
        for side in range(4):
            base = (y * G + (quad * 4 + side) * 8) * G
            for r in range(0, G, 8):
                copies = spread_groups(out[r : r + 8, side * LANES : (side + 1) * LANES], (8, LANES))
                for xl in range(8):
                    dense[pl.ds(pl.multiple_of(base + xl * G + r, 8), 8), :] = copies[xl]
        return carry

    lax.fori_loop(0, GY * 3, along_z, 0)
    masks = source_masks()

    def pick(i, carry):
        for j in range(16):
            k = i * 16 + j
            row = dense[pl.ds(cells[k], 1), :]
            for s in range(1, BD):
                row = jnp.where(masks[s], dense[pl.ds(cells[s * KW + k], 1), :], row)
            turned[pl.ds(k, 1), :] = row
        return carry

    lax.fori_loop(0, KW // 16, pick, 0)

    def turn(i, carry):
        at = pl.multiple_of(i * LANES, LANES)
        terms[:, pl.ds(at, LANES)] = turned[pl.ds(at, LANES), :].T
        return carry

    lax.fori_loop(0, KW // LANES, turn, 0)


def pullback_kernel(grads, s, y0, y1, y2, y3, z1, z2, z3, z4, t1, t2, t3, t4, coefs, first, out):
    def mul(a, b):
        return jnp.dot(a[...], b[...], precision=highest, preferred_element_type=f32)

    y, z, t = (y0, y1, y2, y3), (None, z1, z2, z3, z4), (None, t1, t2, t3, t4)
    values = s[...]
    squared = jnp.sum(values * values, keepdims=True)
    frob = jnp.sqrt(squared)
    root = jnp.sqrt(frob)
    given = grads[...]
    zb = given / root
    fb = -0.5 * jnp.sum(given * z4[...], keepdims=True) / (frob * root)
    yb = None
    for k in range(NS_ITERS, 0, -1):
        tb = zb if k == 1 else mul(zb, z[k - 1])
        if yb is not None:
            tb = tb + mul(y[k - 1], yb)
        before = tb if k == 1 else mul(z[k - 1], tb)
        before = -0.5 * before
        if yb is not None:
            before = before + mul(yb, t[k])
        if k > 1:
            zb = mul(t[k], zb) - 0.5 * mul(tb, y[k - 1])
        yb = before
    fb = fb - jnp.sum(yb * values, keepdims=True) / squared
    grad = yb / frob + fb * (values / frob)
    both = split((grad + grad.T) / NPW)
    for at in range(0, KW, 512):
        part = pl.ds(at, 512)
        out[:, part] = first[:, part] + dot3(both, split(coefs[:, part]))


def products_kernel(terms, rotated, coefs, kinetic, occupancy, grads, sums):
    added = jnp.zeros((NB, NB), f32)

    def dot_t(a, b):
        return lax.dot_general(a, b, (((1,), (1,)), ((), ())), preferred_element_type=f32)

    for at in range(0, KW, 512):
        part = pl.ds(at, 512)
        value = occupancy[...] * (kinetic[:, part] * rotated[:, part] + terms[:, part])
        grads[:, part] = value
        a, b = split(coefs[:, part]), split(value)
        added = added + (dot_t(a[0], b[0]) + (dot_t(a[0], b[1]) + dot_t(a[1], b[0])))
    sums[...] = added


def call(kernel, out_shapes, scratch, scalars, *operands, unread=()):
    vmem = pl.BlockSpec(memory_space=pltpu.VMEM)
    smem = pl.BlockSpec(memory_space=pltpu.SMEM)
    return pl.pallas_call(
        kernel,
        out_shape=out_shapes,
        in_specs=[smem] * scalars
        + [vmem] * (len(operands) - scalars)
        + [pl.BlockSpec(memory_space=pl.ANY)] * len(unread),
        out_specs=jax.tree.map(lambda _: vmem, out_shapes),
        scratch_shapes=scratch,
        compiler_params=pltpu.CompilerParams(vmem_limit_bytes=58 * 1024 * 1024),
    )(*operands, *unread)


def array(*shape):
    return jax.ShapeDtypeStruct(shape, f32)


def matmul(left_side, right_side):
    return jnp.dot(left_side, right_side, precision=highest, preferred_element_type=f32)


def loewdin(intersection):
    frob_norm = jnp.sqrt(jnp.sum(intersection * intersection))
    identity = jnp.eye(intersection.shape[0], dtype=f32)
    ys, zs, ts = [intersection / frob_norm], [], []
    for repeat in range(NS_ITERS):
        product = matmul(zs[-1], ys[-1]) if zs else ys[-1]
        ts.append(1.5 * identity - 0.5 * product)
        zs.append(matmul(ts[-1], zs[-1]) if zs else ts[-1])
        if repeat < NS_ITERS - 1:
            ys.append(matmul(ys[-1], ts[-1]))
    return zs[-1] / jnp.sqrt(frob_norm), (*ys, *zs, *ts)


def total(values):
    axes = ("pw", "band")
    pieces = lax.all_to_all(values, axes, split_axis=0, concat_axis=0, tiled=True)
    row = jnp.sum(pieces, axis=0, keepdims=True)
    copies = jnp.broadcast_to(row, values.shape)
    return lax.all_to_all(copies, axes, split_axis=0, concat_axis=0, tiled=True)


def band_total(values):
    values = values + lax.ppermute(values, "band", [(i, i ^ 1) for i in range(BD)])
    others = [lax.ppermute(values, "band", [(i, (i + 2 * step) % BD) for i in range(BD)]) for step in (1, 2, 3)]
    return values + ((others[0] + others[2]) + others[1])


def packings():
    chosen = np.zeros((PARTS, 2, G, LANES))
    packed = np.zeros((PARTS, 2, WIDE, LANES))
    for part in range(PARTS):
        blocks = [m for pair in BLOCKS[part * PAIRS : (part + 1) * PAIRS] for m in pair]
        for half in range(2):
            for i, m in enumerate(blocks):
                for q in range(BD):
                    lane = half * 64 + i * BD + q
                    chosen[part, half, m + 12 * q, lane] = 1
                    row = i * LANES + q * LB
                    packed[part, half, row : row + LB, lane] = 1
    return chosen, packed


def to_sums(planes, chosen):
    values = planes.reshape(GY, 2, HALF, G)
    packed = matmul(values[:, 0], chosen[0]) + matmul(values[:, 1], chosen[1])
    return packed.reshape(SUM_ROWS, LANES)


def from_sums(parts, chosen):
    halves_of_y = [
        sum(matmul(parts[part], chosen[part, half].T) for part in range(PARTS)).reshape(GY, 1, HALF, G)
        for half in range(2)
    ]
    return jnp.concatenate(halves_of_y, axis=1).reshape(GY, G * G)


def shards(coefficients, occupancy, kinetic, cell_map, potential_ext, core_density):
    table = tables()
    chosen, packed = packings()
    chosen = chosen.astype(np.float32)
    pack = packed[0].astype(ml_dtypes.bfloat16)
    unpack = np.swapaxes(pack, 1, 2)
    unused = (1.0 - chosen.sum(axis=(1, 2))).astype(np.float32)
    pw_pos = lax.axis_index("pw")
    band_pos = lax.axis_index("band")
    cells = cell_map - pw_pos * SLAB
    share = lax.dynamic_slice_in_dim(occupancy / NB, band_pos * LB, LB)
    share = jnp.tile(share, XB * BD).reshape(1, WIDE)
    core = [to_sums(core_density, chosen[part]) + unused[part] for part in range(PARTS)]
    external = [to_sums(potential_ext, chosen[part]) for part in range(PARTS)]

    intersection = total(matmul(coefficients, coefficients.T)) / NPW
    weights, iterates = loewdin(intersection)
    rotated = matmul(weights.T, coefficients)
    block = lax.all_to_all(rotated, "band", split_axis=0, concat_axis=0, tiled=True)
    sent = call(
        scatter_kernel,
        [array(ROWS, LANES)] * PARTS,
        [
            pltpu.VMEM((SLAB, LANES), f32),
            pltpu.VMEM((KW, LANES), f32),
            pltpu.VMEM((12, GY * G, LANES), f32),
            pltpu.VMEM((6, GY * G, 2 * LANES), bf16),
            pltpu.VMEM((6, GY * G, 2 * LANES), bf16),
        ],
        1,
        cells,
        block,
        table["z_out"],
        *table["mix"],
        unread=(*core, *external),
    )
    exchange = functools.partial(lax.all_to_all, axis_name="pw", split_axis=0, concat_axis=0, tiled=True)
    density, returned, after = [], [], []
    for part in range(PARTS):
        received = exchange(sent[part])
        fields, sums = call(
            density_kernel,
            (array(ROWS, LANES), array(SUM_ROWS, LANES)),
            [],
            0,
            received,
            table["y_out"],
            *pack,
            share,
            unread=after,
        )
        density.append(core[part] + band_total(sums))
        product = call(
            potential_kernel,
            array(ROWS, LANES),
            [],
            0,
            density[part],
            external[part],
            fields,
            table["y_in"],
            *unpack,
        )
        after = [product]
        returned.append(exchange(product))
    terms = call(
        gather_kernel,
        array(NB, KW),
        [
            pltpu.VMEM((SLAB, LANES), f32),
            pltpu.VMEM((KW, LANES), f32),
            pltpu.VMEM((6, GY * G, 2 * LANES), f32),
            pltpu.VMEM((3, GY * G, 4 * LANES), bf16),
            pltpu.VMEM((3, GY * G, 4 * LANES), bf16),
        ],
        1,
        cells,
        *returned,
        table["z_in"],
        *table["mix_t"],
    )
    row_term = lax.all_to_all(terms, "band", split_axis=0, concat_axis=0, tiled=True)
    grad_rotated, partial = call(
        products_kernel,
        (array(NB, KW), array(NB, NB)),
        [],
        0,
        row_term,
        rotated,
        coefficients,
        kinetic.reshape(1, KW),
        occupancy.reshape(NB, 1),
    )
    grad_weights = total(partial)
    first = matmul(weights, grad_rotated)
    grad_coef = call(
        pullback_kernel, array(NB, KW), [], 0, grad_weights, intersection, *iterates, coefficients, first
    )
    return (grad_coef, from_sums(density, chosen))


def solution(mesh):
    placed = (
        P(None, ("pw", "band")),
        P(),
        P(("pw", "band")),
        P("pw"),
        P("pw", None),
        P("pw", None),
    )
    return jax.shard_map(
        shards,
        mesh=mesh,
        in_specs=placed,
        out_specs=(P(None, ("pw", "band")), P("pw", None)),
        check_vma=False,
    )
```

```python
import functools
import math

import jax
import jax.numpy as jnp
import ml_dtypes
import numpy as np
from jax import lax
from jax.experimental import pallas as pl
from jax.experimental.pallas import tpu as pltpu
from jax.sharding import PartitionSpec as P

G = 96
NPW = 393216
NB = 128
NS_ITERS = 4
PW = 16
BD = 8
LB = NB // BD
GY = G // PW
ORDER = (0, 1, 2, 6, 3, 7, 4, 5)
HELD = BD // 2
PARTS = 2
BLOCKS = ((0, 6), (1, 11), (2, 10), (3, 9), (4, 8), (5, 7))
PAIRS = len(BLOCKS) // PARTS
XB = 2 * PAIRS
COLS = GY * XB
HALF = G // 2
WIDE = XB * 128
SLAB = GY * G * G
KW = NPW // (PW * BD)
BLK = GY * COLS
ROWS = PW * BLK
SUM_ROWS = GY * HALF
LANES = 128

highest = lax.Precision.HIGHEST
slater = 0.9847450218426965
bf16 = jnp.bfloat16
f32 = jnp.float32


def halves(table):
    high = table.astype(ml_dtypes.bfloat16)
    low = (table - high.astype(np.float64)).astype(ml_dtypes.bfloat16)
    return high, low


def tables():
    counter = np.arange(G)
    phases = 2.0 * np.pi / G * (counter[:, None] * counter[None, :] % G)
    cas = np.cos(phases) + np.sin(phases)
    order = (np.arange(PW)[None, :] * GY + np.arange(GY)[:, None]).reshape(-1)
    scaled = cas / math.sqrt(NPW)
    mixes = []
    small = np.arange(8)

    def mix(m):
        beta = 2.0 * np.pi / G * (small[:, None] * (m + 12 * small[None, :]))
        even = np.kron(np.cos(beta) + np.sin(beta), np.eye(LB))
        odd = np.kron(np.cos(beta) - np.sin(beta), np.eye(LB))
        return even, odd

    zero = np.zeros((LANES, LANES))
    mixes.append(np.block([[mix(0)[0], zero], [zero, mix(6)[0]]]))
    for m in range(1, 6):
        here, there = mix(m), mix(12 - m)
        mixes.append(np.block([[here[0], there[0]], [here[1], -there[1]]]))
    mixes = np.stack(mixes)
    return dict(
        z_out=np.concatenate(halves(scaled[order, :])),
        y_out=np.concatenate(halves(cas[:, order])),
        y_in=np.concatenate(halves(cas[order, :])),
        z_in=np.concatenate(halves(scaled[:, order])),
        mix=halves(mixes),
        mix_t=halves(np.swapaxes(mixes, 1, 2)),
    )


ROOT3 = math.sqrt(3.0) / 2.0


def cos12(e):
    a0, a1, a2 = e[0] + e[6], e[1] + e[5], e[2] + e[4]
    b0, b1, b2 = e[0] - e[6], e[1] - e[5], e[2] - e[4]
    t = ROOT3 * b1
    h = b0 + 0.5 * b2
    r = 0.5 * (a1 + a2)
    d = 0.5 * (a1 - a2)
    return [
        a0 + a1 + a2 + e[3],
        h + t,
        a0 + d - e[3],
        b0 - b2,
        a0 - r + e[3],
        h - t,
        a0 - a1 + a2 - e[3],
    ]


def sin12(o):
    p1, p2 = o[1] + o[5], o[2] + o[4]
    r1, r2 = o[1] - o[5], o[2] - o[4]
    h = 0.5 * p1 + o[3]
    t = ROOT3 * p2
    return [None, h + t, ROOT3 * (r1 + r2), p1 - o[3], ROOT3 * (r1 - r2), h - t]


def split(values):
    high = values.astype(bf16)
    return high, (values - high.astype(f32)).astype(bf16)


def dot(a, b):
    return jnp.dot(a, b, preferred_element_type=f32)


def dot3(a, b):
    return dot(a[0], b[0]) + (dot(a[0], b[1]) + dot(a[1], b[0]))


def transform(table, b):
    rows = table.shape[0] // 2
    both = dot(table, b[0])
    return both[:rows] + (dot(table[:rows], b[1]) + both[rows:])


def lane_bit(shape, bit):
    return (lax.broadcasted_iota(jnp.int32, shape, 1) & bit) == 0


def gather_groups(parts, shape):
    for width in (16, 32, 64):
        first = lane_bit(shape, width)
        parts = [
            jnp.where(first, a, b) + pltpu.roll(jnp.where(first, b, a), width, 1)
            for a, b in zip(parts[0::2], parts[1::2])
        ]
    return parts[0]


def spread_groups(value, shape):
    parts = [value]
    for width in (64, 32, 16):
        first = lane_bit(shape, width)
        turned = [pltpu.roll(part, width, 1) for part in parts]
        parts = [
            side
            for part, turn in zip(parts, turned)
            for side in (jnp.where(first, part, turn), jnp.where(first, turn, part))
        ]
    return parts


def lines(ref, start):
    return jnp.concatenate([ref[pl.ds(row, PW, stride=BLK), :] for row in start], axis=0)


def source_masks():
    group = lax.broadcasted_iota(jnp.int32, (1, LANES), 1) // LB
    return [group == s for s in range(BD)]


def clear_kernel(unread, dense):
    zero = jnp.zeros((256, LANES), f32)

    def clear(i, carry):
        dense[pl.ds(pl.multiple_of(i * 256, 256), 256), :] = zero
        return carry

    lax.fori_loop(0, SLAB // 256, clear, 0)


def place_kernel(first, cells, *rest):
    blocks, (dense, turned) = rest[:HELD], rest[-2:]
    empty = jnp.zeros((HELD * LB, LANES), f32)

    def turn(i, carry):
        at = pl.multiple_of(i * LANES, LANES)
        rows = [block[:, pl.ds(at, LANES)] for block in blocks]
        rows = [empty, *rows] if first else [*rows, empty]
        turned[pl.ds(at, LANES), :] = jnp.concatenate(rows, axis=0).T
        return carry

    lax.fori_loop(0, KW // LANES, turn, 0)
    masks = source_masks()

    def place(i, carry):
        for j in range(16):
            k = i * 16 + j
            row = turned[pl.ds(k, 1), :]
            for p in range(HELD):
                pltpu.store(dense.at[pl.ds(cells[p * KW + k], 1), :], row, mask=masks[first + p])
        return carry

    lax.fori_loop(0, KW // 16, place, 0)


def fold_kernel(cells, *rest):
    given, zt, mh, ml, dense, sent0, sent1, turned, fields, high, low = rest[HELD:]
    place_kernel(HELD, cells, *rest[:HELD], dense, turned)
    table = zt[...]

    def along_z(i, carry):
        y, quad = i // 3, i % 3
        folded = []
        for side in range(4):
            base = (y * G + (quad * 4 + side) * 8) * G
            tiles = []
            for r in range(0, G, 8):
                parts = [dense[pl.ds(pl.multiple_of(base + xl * G + r, 8), 8), :] for xl in range(8)]
                tiles.append(gather_groups(parts, (8, LANES)))
            folded.append(jnp.concatenate(tiles, axis=0))
        out = transform(table, split(jnp.concatenate(folded, axis=1)))
        at = pl.multiple_of(y * G, G)
        for side in range(4):
            fields[quad * 4 + side, pl.ds(at, G), :] = out[:, side * LANES : (side + 1) * LANES]
        return carry

    lax.fori_loop(0, GY * 3, along_z, 0)

    def twelve(i, carry):
        at = pl.multiple_of(i * 16, 16)
        e = [fields[xh, pl.ds(at, 16), :] for xh in range(12)]
        c = cos12([e[0]] + [e[j] + e[12 - j] for j in range(1, 6)] + [e[6]])
        s = sin12([None] + [e[j] - e[12 - j] for j in range(1, 6)])
        for p in range(6):
            high[p, pl.ds(at, 16), :], low[p, pl.ds(at, 16), :] = split(
                jnp.concatenate([c[p], c[6] if p == 0 else s[p]], axis=1)
            )
        return carry

    lax.fori_loop(0, GY * G // 16, twelve, 0)
    for p in range(2 * PAIRS):
        out = dot3((high[p], low[p]), (mh[p], ml[p]))
        sent = (sent0, sent1)[p // PAIRS]
        for side in range(2):
            for y in range(GY):
                for z in range(GY):
                    at = y * G + z * PW
                    sent[pl.ds(y * COLS + z * XB + p % PAIRS * 2 + side, PW, stride=BLK), :] = out[
                        at : at + PW, side * LANES : (side + 1) * LANES
                    ]


def density_kernel(recv, yt, pack0, pack1, share, *rest):
    fields, sums = rest[-2:]
    table = yt[...]
    weight = share[...]

    def along_y(z, carry):
        data = [lines(recv, [y * COLS + z * XB + i for y in range(GY)]) for i in range(XB)]
        out = transform(table, split(jnp.concatenate(data, axis=1)))
        for i in range(XB):
            at = pl.multiple_of((z * XB + i) * G, G)
            fields[pl.ds(at, G), :] = out[:, i * LANES : (i + 1) * LANES]
        high, low = split(weight * out * out)
        first, second = pack0[...], pack1[...]
        added = dot(high[:HALF], first) + dot(low[:HALF], first)
        added = added + (dot(high[HALF:], second) + dot(low[HALF:], second))
        sums[pl.ds(pl.multiple_of(z * HALF, HALF), HALF), :] = added
        return carry

    lax.fori_loop(0, GY, along_y, 0)


def potential_kernel(density, external, fields, yt, open0, open1, sent):
    table = yt[...]

    def along_y(z, carry):
        at = pl.multiple_of(z * HALF, HALF)
        dens = density[pl.ds(at, HALF), :]
        root = jnp.exp(jnp.log(dens) * (1.0 / 3.0))
        root = root - (root - dens / (root * root)) * (1.0 / 3.0)
        high, low = split(external[pl.ds(at, HALF), :] - slater * root)
        first, second = open0[...], open1[...]
        spread = [dot(high, first) + dot(low, first), dot(high, second) + dot(low, second)]
        value = [fields[pl.ds(pl.multiple_of((z * XB + i) * G, G), G), :] for i in range(XB)]
        product = jnp.concatenate(spread, axis=0) * jnp.concatenate(value, axis=1)
        out = transform(table, split(product))
        for i in range(XB):
            for y in range(GY):
                sent[pl.ds(y * COLS + z * XB + i, PW, stride=BLK), :] = out[
                    y * PW : (y + 1) * PW, i * LANES : (i + 1) * LANES
                ]
        return carry

    lax.fori_loop(0, GY, along_y, 0)


def spread_kernel(recv0, recv1, zt, mh, ml, dense, uv, bh, bl):
    table = zt[...]
    for p in range(2 * PAIRS):
        recv = (recv0, recv1)[p // PAIRS]
        starts = [y * COLS + z * XB + p % PAIRS * 2 for y in range(GY) for z in range(GY)]
        data = [lines(recv, [row + side for row in starts]) for side in range(2)]
        uv[p] = dot3(split(jnp.concatenate(data, axis=1)), (mh[p], ml[p]))

    def twelve(i, carry):
        at = pl.multiple_of(i * 16, 16)
        left = [uv[p, pl.ds(at, 16), :LANES] for p in range(6)]
        right = [uv[p, pl.ds(at, 16), LANES:] for p in range(6)]
        c, s = cos12(left + [right[0]]), sin12([None] + right[1:])
        x = [c[0]] + [c[j] + s[j] for j in range(1, 6)] + [c[6]] + [c[j] - s[j] for j in range(5, 0, -1)]
        for quad in range(3):
            high, low = split(jnp.concatenate(x[4 * quad : 4 * quad + 4], axis=1))
            bh[quad, pl.ds(at, 16), :] = high
            bl[quad, pl.ds(at, 16), :] = low
        return carry

    lax.fori_loop(0, GY * G // 16, twelve, 0)

    def along_z(i, carry):
        y, quad = i // 3, i % 3
        at = pl.multiple_of(y * G, G)
        out = transform(table, (bh[quad, pl.ds(at, G), :], bl[quad, pl.ds(at, G), :]))
        for side in range(4):
            base = (y * G + (quad * 4 + side) * 8) * G
            for r in range(0, G, 8):
                copies = spread_groups(out[r : r + 8, side * LANES : (side + 1) * LANES], (8, LANES))
                for xl in range(8):
                    dense[pl.ds(pl.multiple_of(base + xl * G + r, 8), 8), :] = copies[xl]
        return carry

    lax.fori_loop(0, GY * 3, along_z, 0)


def pick_kernel(first, cells, dense, *rest):
    terms, turned = rest[-1 - HELD : -1], rest[-1]
    masks = source_masks()

    def pick(i, carry):
        for j in range(16):
            k = i * 16 + j
            row = dense[pl.ds(cells[k], 1), :]
            for p in range(1, HELD):
                row = jnp.where(masks[first + p], dense[pl.ds(cells[p * KW + k], 1), :], row)
            turned[pl.ds(k, 1), :] = row
        return carry

    lax.fori_loop(0, KW // 16, pick, 0)

    def turn(i, carry):
        at = pl.multiple_of(i * LANES, LANES)
        rows = turned[pl.ds(at, LANES), :].T
        for p in range(HELD):
            terms[p][:, pl.ds(at, LANES)] = rows[(first + p) * LB : (first + p + 1) * LB]
        return carry

    lax.fori_loop(0, KW // LANES, turn, 0)


def rotate_kernel(order, weights, coefs, *rest):
    blocks, rotated = rest[-1 - BD : -1], rest[-1]
    turned = split(weights[...].T)
    for at in range(0, KW, 512):
        part = pl.ds(at, 512)
        rotated[:, part] = dot3(turned, split(coefs[:, part]))
    for p in range(BD):
        blocks[p][...] = rotated[pl.ds(pl.multiple_of(order[p] * LB, LB), LB), :]


def pullback_kernel(grads, s, y0, y1, y2, y3, z1, z2, z3, z4, t1, t2, t3, t4, coefs, first, out):
    def mul(a, b):
        return jnp.dot(a[...], b[...], precision=highest, preferred_element_type=f32)

    y, z, t = (y0, y1, y2, y3), (None, z1, z2, z3, z4), (None, t1, t2, t3, t4)
    values = s[...]
    squared = jnp.sum(values * values, keepdims=True)
    frob = jnp.sqrt(squared)
    root = jnp.sqrt(frob)
    given = grads[...]
    zb = given / root
    fb = -0.5 * jnp.sum(given * z4[...], keepdims=True) / (frob * root)
    yb = None
    for k in range(NS_ITERS, 0, -1):
        tb = zb if k == 1 else mul(zb, z[k - 1])
        if yb is not None:
            tb = tb + mul(y[k - 1], yb)
        before = tb if k == 1 else mul(z[k - 1], tb)
        before = -0.5 * before
        if yb is not None:
            before = before + mul(yb, t[k])
        if k > 1:
            zb = mul(t[k], zb) - 0.5 * mul(tb, y[k - 1])
        yb = before
    fb = fb - jnp.sum(yb * values, keepdims=True) / squared
    grad = yb / frob + fb * (values / frob)
    both = split((grad + grad.T) / NPW)
    for at in range(0, KW, 512):
        part = pl.ds(at, 512)
        out[:, part] = first[:, part] + dot3(both, split(coefs[:, part]))


def products_kernel(order, *rest):
    terms, rotated, (coefs, kinetic, occupancy, grads, sums) = rest[:BD], rest[BD : 2 * BD], rest[2 * BD :]
    for p in range(BD):
        rows = pl.ds(pl.multiple_of(order[p] * LB, LB), LB)
        grads[rows, :] = occupancy[rows, :] * (kinetic[...] * rotated[p][...] + terms[p][...])
    added = jnp.zeros((NB, NB), f32)

    def dot_t(a, b):
        return lax.dot_general(a, b, (((1,), (1,)), ((), ())), preferred_element_type=f32)

    for at in range(0, KW, 512):
        part = pl.ds(at, 512)
        a, b = split(coefs[:, part]), split(grads[:, part])
        added = added + (dot_t(a[0], b[0]) + (dot_t(a[0], b[1]) + dot_t(a[1], b[0])))
    sums[...] = added


def call(kernel, out_shapes, scratch, scalars, *operands, unread=(), alias=None, room=58, micros=3):
    vmem = pl.BlockSpec(memory_space=pltpu.VMEM)
    smem = pl.BlockSpec(memory_space=pltpu.SMEM)
    return pl.pallas_call(
        kernel,
        out_shape=out_shapes,
        in_specs=[smem] * scalars
        + [vmem] * (len(operands) - scalars)
        + [pl.BlockSpec(memory_space=pl.ANY)] * len(unread),
        out_specs=jax.tree.map(lambda _: vmem, out_shapes),
        scratch_shapes=scratch,
        input_output_aliases=alias or {},
        cost_estimate=pl.CostEstimate(flops=0, bytes_accessed=micros * 3_500_000, transcendentals=0),
        compiler_params=pltpu.CompilerParams(vmem_limit_bytes=room * 1024 * 1024),
    )(*operands, *unread)


def kept(*shape):
    return pltpu.VMEM(shape, f32)


def held(values):
    return pltpu.with_memory_space_constraint(values, pltpu.VMEM)


def array(*shape):
    return jax.ShapeDtypeStruct(shape, f32)


def matmul(left_side, right_side):
    return jnp.dot(left_side, right_side, precision=highest, preferred_element_type=f32)


def loewdin(intersection):
    frob_norm = jnp.sqrt(jnp.sum(intersection * intersection))
    identity = jnp.eye(intersection.shape[0], dtype=f32)
    ys, zs, ts = [intersection / frob_norm], [], []
    for repeat in range(NS_ITERS):
        product = matmul(zs[-1], ys[-1]) if zs else ys[-1]
        ts.append(1.5 * identity - 0.5 * product)
        zs.append(matmul(ts[-1], zs[-1]) if zs else ts[-1])
        if repeat < NS_ITERS - 1:
            ys.append(matmul(ys[-1], ts[-1]))
    return zs[-1] / jnp.sqrt(frob_norm), (*ys, *zs, *ts)


def total(values):
    axes = ("pw", "band")
    pieces = lax.all_to_all(values, axes, split_axis=0, concat_axis=0, tiled=True)
    row = jnp.sum(pieces, axis=0, keepdims=True)
    copies = jnp.broadcast_to(row, values.shape)
    return lax.all_to_all(copies, axes, split_axis=0, concat_axis=0, tiled=True)


def band_total(values):
    values = values + lax.ppermute(values, "band", [(i, i ^ 1) for i in range(BD)])
    others = [lax.ppermute(values, "band", [(i, (i + 2 * step) % BD) for i in range(BD)]) for step in (1, 2, 3)]
    return values + ((others[0] + others[2]) + others[1])


def packings():
    chosen = np.zeros((PARTS, 2, G, LANES))
    packed = np.zeros((PARTS, 2, WIDE, LANES))
    for part in range(PARTS):
        blocks = [m for pair in BLOCKS[part * PAIRS : (part + 1) * PAIRS] for m in pair]
        for half in range(2):
            for i, m in enumerate(blocks):
                for q in range(BD):
                    lane = half * 64 + i * BD + q
                    chosen[part, half, m + 12 * q, lane] = 1
                    row = i * LANES + q * LB
                    packed[part, half, row : row + LB, lane] = 1
    return chosen, packed


def to_sums(planes, chosen):
    values = planes.reshape(GY, 2, HALF, G)
    packed = matmul(values[:, 0], chosen[0]) + matmul(values[:, 1], chosen[1])
    return packed.reshape(SUM_ROWS, LANES)


def from_sums(parts, chosen):
    halves_of_y = [
        sum(matmul(parts[part], chosen[part, half].T) for part in range(PARTS)).reshape(GY, 1, HALF, G)
        for half in range(2)
    ]
    return jnp.concatenate(halves_of_y, axis=1).reshape(GY, G * G)


def shards(coefficients, occupancy, kinetic, cell_map, potential_ext, core_density):
    table = tables()
    chosen, packed = packings()
    chosen = chosen.astype(np.float32)
    pack = packed[0].astype(ml_dtypes.bfloat16)
    unpack = np.swapaxes(pack, 1, 2)
    unused_lanes = (1.0 - chosen.sum(axis=(1, 2))).astype(np.float32)
    pw_pos = lax.axis_index("pw")
    band_pos = lax.axis_index("band")
    cells = cell_map - pw_pos * SLAB

    order = jnp.bitwise_xor(band_pos, jnp.asarray(ORDER, jnp.int32))
    cells = [lax.dynamic_slice_in_dim(cells, order[p] * KW, KW) for p in range(BD)]
    cells = [jnp.concatenate(cells[:HELD]), jnp.concatenate(cells[HELD:])]

    def meet(block, p):
        if ORDER[p] == 0:
            return block
        return lax.ppermute(block, "band", [(i, i ^ ORDER[p]) for i in range(BD)])

    intersection = total(matmul(coefficients, coefficients.T)) / NPW
    weights, iterates = loewdin(intersection)
    rotated = call(
        rotate_kernel,
        [array(LB, KW)] * BD,
        [pltpu.VMEM((NB, KW), f32)],
        1,
        order,
        weights,
        coefficients,
        unread=cells,
        room=28,
    )
    near = [meet(rotated[p], p) for p in range(HELD)]
    dense = call(clear_kernel, kept(SLAB, LANES), [], 0, unread=(rotated[0],), room=28)
    *barred, dense = lax.optimization_barrier((*near, *rotated[HELD:], dense))
    blocks = [*barred[:HELD], *(meet(barred[p], p) for p in range(HELD, BD))]
    dense = call(
        functools.partial(place_kernel, 0),
        kept(SLAB, LANES),
        [pltpu.VMEM((KW, LANES), f32)],
        1,
        cells[0],
        *blocks[:HELD],
        held(dense),
        alias={1 + HELD: 0},
        room=28,
        micros=14,
    )
    halves_shape = (2 * PAIRS, GY * G, 2 * LANES)
    unused, *sent = call(
        fold_kernel,
        (kept(SLAB, LANES), array(ROWS, LANES), array(ROWS, LANES)),
        [
            pltpu.VMEM((KW, LANES), f32),
            pltpu.VMEM((12, GY * G, LANES), f32),
            pltpu.VMEM(halves_shape, bf16),
            pltpu.VMEM(halves_shape, bf16),
        ],
        1,
        cells[1],
        *blocks[HELD:],
        held(dense),
        table["z_out"],
        *table["mix"],
        alias={1 + HELD: 0},
        room=28,
        micros=29,
    )
    *sent, core_density, potential_ext, kinetic, occupancy = lax.optimization_barrier(
        (*sent, core_density, potential_ext, kinetic, occupancy)
    )
    core = [to_sums(core_density, chosen[part]) + unused_lanes[part] for part in range(PARTS)]
    external = [to_sums(potential_ext, chosen[part]) for part in range(PARTS)]
    share = lax.dynamic_slice_in_dim(occupancy / NB, band_pos * LB, LB)
    share = jnp.tile(share, XB * BD).reshape(1, WIDE)
    kinetic_row = kinetic.reshape(1, KW)
    occupancy_column = occupancy.reshape(NB, 1)
    exchange = functools.partial(lax.all_to_all, axis_name="pw", split_axis=0, concat_axis=0, tiled=True)
    density, returned, after = [], [], [*core, *external]
    for part in range(PARTS):
        received = exchange(sent[part])
        fields, sums = call(
            density_kernel,
            (array(ROWS, LANES), array(SUM_ROWS, LANES)),
            [],
            0,
            received,
            table["y_out"],
            *pack,
            share,
            unread=after,
        )
        density.append(core[part] + band_total(sums))
        product = call(
            potential_kernel,
            array(ROWS, LANES),
            [],
            0,
            density[part],
            external[part],
            fields,
            table["y_in"],
            *unpack,
        )
        after = [product]
        returned.append(exchange(product))
    dense = call(
        spread_kernel,
        kept(SLAB, LANES),
        [
            pltpu.VMEM((6, GY * G, 2 * LANES), f32),
            pltpu.VMEM((3, GY * G, 4 * LANES), bf16),
            pltpu.VMEM((3, GY * G, 4 * LANES), bf16),
        ],
        0,
        *returned,
        table["z_in"],
        *table["mix_t"],
        room=28,
        micros=13,
    )
    terms, after = [None, None], ()
    for side in (1, 0):
        terms[side] = call(
            functools.partial(pick_kernel, side * HELD),
            [array(LB, KW)] * HELD,
            [pltpu.VMEM((KW, LANES), f32)],
            1,
            cells[side],
            held(dense),
            unread=after,
            room=28,
            micros=14,
        )
        after = tuple(terms[side])
    far = [meet(terms[1][p], HELD + p) for p in range(HELD)]
    near = terms[0]
    barred = lax.optimization_barrier((*near, *far))
    near, far = barred[:HELD], barred[HELD:]
    terms = [meet(near[p], p) for p in range(HELD)] + list(far)
    grad_rotated, partial = call(
        products_kernel,
        (array(NB, KW), array(NB, NB)),
        [],
        1,
        order,
        *terms,
        *rotated,
        coefficients,
        kinetic_row,
        occupancy_column,
    )
    *density, partial = lax.optimization_barrier((*density, partial))
    grad_weights = total(partial)
    first = matmul(weights, grad_rotated)
    grad_coef = call(
        pullback_kernel, array(NB, KW), [], 0, grad_weights, intersection, *iterates, coefficients, first
    )
    return (grad_coef, from_sums(density, chosen))


def solution(mesh):
    placed = (
        P(None, ("pw", "band")),
        P(),
        P(("pw", "band")),
        P("pw"),
        P("pw", None),
        P("pw", None),
    )
    return jax.shard_map(
        shards,
        mesh=mesh,
        in_specs=placed,
        out_specs=(P(None, ("pw", "band")), P("pw", None)),
        check_vma=False,
    )
```

```python
import functools
import math

import jax
import jax.numpy as jnp
import ml_dtypes
import numpy as np
from jax import lax
from jax.experimental import pallas as pl
from jax.experimental.pallas import tpu as pltpu
from jax.sharding import PartitionSpec as P

G = 96
NPW = 393216
NB = 128
NS_ITERS = 4
PW = 16
BD = 8
LB = NB // BD
GY = G // PW
ORDER = (0, 1, 2, 6, 3, 7, 4, 5)
HELD = BD // 2
FIRST = NPW // (PW * BD) // 2
PARTS = 2
BLOCKS = ((0, 6), (1, 11), (2, 10), (3, 9), (4, 8), (5, 7))
PAIRS = len(BLOCKS) // PARTS
XB = 2 * PAIRS
COLS = GY * XB
HALF = G // 2
WIDE = XB * 128
SLAB = GY * G * G
KW = NPW // (PW * BD)
BLK = GY * COLS
ROWS = PW * BLK
SUM_ROWS = GY * HALF
LANES = 128

highest = lax.Precision.HIGHEST
slater = 0.9847450218426965
bf16 = jnp.bfloat16
f32 = jnp.float32


def halves(table):
    high = table.astype(ml_dtypes.bfloat16)
    low = (table - high.astype(np.float64)).astype(ml_dtypes.bfloat16)
    return high, low


def tables():
    counter = np.arange(G)
    phases = 2.0 * np.pi / G * (counter[:, None] * counter[None, :] % G)
    cas = np.cos(phases) + np.sin(phases)
    order = (np.arange(PW)[None, :] * GY + np.arange(GY)[:, None]).reshape(-1)
    scaled = cas / math.sqrt(NPW)
    mixes = []
    small = np.arange(8)

    def mix(m):
        beta = 2.0 * np.pi / G * (small[:, None] * (m + 12 * small[None, :]))
        even = np.kron(np.cos(beta) + np.sin(beta), np.eye(LB))
        odd = np.kron(np.cos(beta) - np.sin(beta), np.eye(LB))
        return even, odd

    zero = np.zeros((LANES, LANES))
    mixes.append(np.block([[mix(0)[0], zero], [zero, mix(6)[0]]]))
    for m in range(1, 6):
        here, there = mix(m), mix(12 - m)
        mixes.append(np.block([[here[0], there[0]], [here[1], -there[1]]]))
    mixes = np.stack(mixes)
    return dict(
        z_out=np.concatenate(halves(scaled[order, :])),
        y_out=np.concatenate(halves(cas[:, order])),
        y_in=np.concatenate(halves(cas[order, :])),
        z_in=np.concatenate(halves(scaled[:, order])),
        mix=halves(mixes),
        mix_t=halves(np.swapaxes(mixes, 1, 2)),
    )


ROOT3 = math.sqrt(3.0) / 2.0


def cos12(e):
    a0, a1, a2 = e[0] + e[6], e[1] + e[5], e[2] + e[4]
    b0, b1, b2 = e[0] - e[6], e[1] - e[5], e[2] - e[4]
    t = ROOT3 * b1
    h = b0 + 0.5 * b2
    r = 0.5 * (a1 + a2)
    d = 0.5 * (a1 - a2)
    return [
        a0 + a1 + a2 + e[3],
        h + t,
        a0 + d - e[3],
        b0 - b2,
        a0 - r + e[3],
        h - t,
        a0 - a1 + a2 - e[3],
    ]


def sin12(o):
    p1, p2 = o[1] + o[5], o[2] + o[4]
    r1, r2 = o[1] - o[5], o[2] - o[4]
    h = 0.5 * p1 + o[3]
    t = ROOT3 * p2
    return [None, h + t, ROOT3 * (r1 + r2), p1 - o[3], ROOT3 * (r1 - r2), h - t]


def split(values):
    high = values.astype(bf16)
    return high, (values - high.astype(f32)).astype(bf16)


def dot(a, b):
    return jnp.dot(a, b, preferred_element_type=f32)


def dot3(a, b):
    return dot(a[0], b[0]) + (dot(a[0], b[1]) + dot(a[1], b[0]))


def transform(table, b):
    rows = table.shape[0] // 2
    both = dot(table, b[0])
    return both[:rows] + (dot(table[:rows], b[1]) + both[rows:])


def lane_bit(shape, bit):
    return (lax.broadcasted_iota(jnp.int32, shape, 1) & bit) == 0


def gather_groups(parts, shape):
    for width in (16, 32, 64):
        first = lane_bit(shape, width)
        parts = [
            jnp.where(first, a, b) + pltpu.roll(jnp.where(first, b, a), width, 1)
            for a, b in zip(parts[0::2], parts[1::2])
        ]
    return parts[0]


def spread_groups(value, shape):
    parts = [value]
    for width in (64, 32, 16):
        first = lane_bit(shape, width)
        turned = [pltpu.roll(part, width, 1) for part in parts]
        parts = [
            side
            for part, turn in zip(parts, turned)
            for side in (jnp.where(first, part, turn), jnp.where(first, turn, part))
        ]
    return parts


def lines(ref, start):
    return jnp.concatenate([ref[pl.ds(row, PW, stride=BLK), :] for row in start], axis=0)


def source_masks():
    group = lax.broadcasted_iota(jnp.int32, (1, LANES), 1) // LB
    return [group == s for s in range(BD)]


def clear_kernel(unread, dense):
    zero = jnp.zeros((256, LANES), f32)

    def clear(i, carry):
        dense[pl.ds(pl.multiple_of(i * 256, 256), 256), :] = zero
        return carry

    lax.fori_loop(0, SLAB // 256, clear, 0)


def place_kernel(cells, *rest):
    blocks, (dense, turned) = rest[:HELD], rest[-2:]

    def turn(i, carry):
        at = pl.multiple_of(i * LANES, LANES)
        rows = [block[:, pl.ds(half * FIRST + at, LANES)] for half in range(2) for block in blocks]
        turned[pl.ds(at, LANES), :] = jnp.concatenate(rows, axis=0).T
        return carry

    lax.fori_loop(0, FIRST // LANES, turn, 0)
    masks = source_masks()

    def place(i, carry):
        for j in range(16):
            k = i * 16 + j
            row = turned[pl.ds(k, 1), :]
            for group in range(BD):
                half, p = group // HELD, group % HELD
                cell = cells[p * KW + half * FIRST + k]
                pltpu.store(dense.at[pl.ds(cell, 1), :], row, mask=masks[group])
        return carry

    lax.fori_loop(0, FIRST // 16, place, 0)


def fold_kernel(cells, *rest):
    given, zt, mh, ml, dense, sent0, sent1, turned, fields, high, low = rest[HELD:]
    place_kernel(cells, *rest[:HELD], dense, turned)
    table = zt[...]

    def along_z(i, carry):
        y, quad = i // 3, i % 3
        folded = []
        for side in range(4):
            base = (y * G + (quad * 4 + side) * 8) * G
            tiles = []
            for r in range(0, G, 8):
                parts = [dense[pl.ds(pl.multiple_of(base + xl * G + r, 8), 8), :] for xl in range(8)]
                tiles.append(gather_groups(parts, (8, LANES)))
            folded.append(jnp.concatenate(tiles, axis=0))
        out = transform(table, split(jnp.concatenate(folded, axis=1)))
        at = pl.multiple_of(y * G, G)
        for side in range(4):
            fields[quad * 4 + side, pl.ds(at, G), :] = out[:, side * LANES : (side + 1) * LANES]
        return carry

    lax.fori_loop(0, GY * 3, along_z, 0)

    def twelve(i, carry):
        at = pl.multiple_of(i * 16, 16)
        e = [fields[xh, pl.ds(at, 16), :] for xh in range(12)]
        c = cos12([e[0]] + [e[j] + e[12 - j] for j in range(1, 6)] + [e[6]])
        s = sin12([None] + [e[j] - e[12 - j] for j in range(1, 6)])
        for p in range(6):
            high[p, pl.ds(at, 16), :], low[p, pl.ds(at, 16), :] = split(
                jnp.concatenate([c[p], c[6] if p == 0 else s[p]], axis=1)
            )
        return carry

    lax.fori_loop(0, GY * G // 16, twelve, 0)
    for p in range(2 * PAIRS):
        out = dot3((high[p], low[p]), (mh[p], ml[p]))
        sent = (sent0, sent1)[p // PAIRS]
        for side in range(2):
            for y in range(GY):
                for z in range(GY):
                    at = y * G + z * PW
                    sent[pl.ds(y * COLS + z * XB + p % PAIRS * 2 + side, PW, stride=BLK), :] = out[
                        at : at + PW, side * LANES : (side + 1) * LANES
                    ]


def density_kernel(recv, yt, pack0, pack1, share, *rest):
    fields, sums = rest[-2:]
    table = yt[...]
    weight = share[...]

    def along_y(z, carry):
        data = [lines(recv, [y * COLS + z * XB + i for y in range(GY)]) for i in range(XB)]
        out = transform(table, split(jnp.concatenate(data, axis=1)))
        for i in range(XB):
            at = pl.multiple_of((z * XB + i) * G, G)
            fields[pl.ds(at, G), :] = out[:, i * LANES : (i + 1) * LANES]
        high, low = split(weight * out * out)
        first, second = pack0[...], pack1[...]
        added = dot(high[:HALF], first) + dot(low[:HALF], first)
        added = added + (dot(high[HALF:], second) + dot(low[HALF:], second))
        sums[pl.ds(pl.multiple_of(z * HALF, HALF), HALF), :] = added
        return carry

    lax.fori_loop(0, GY, along_y, 0)


def potential_kernel(density, external, fields, yt, open0, open1, sent):
    table = yt[...]

    def along_y(z, carry):
        at = pl.multiple_of(z * HALF, HALF)
        dens = density[pl.ds(at, HALF), :]
        root = jnp.exp(jnp.log(dens) * (1.0 / 3.0))
        root = root - (root - dens / (root * root)) * (1.0 / 3.0)
        high, low = split(external[pl.ds(at, HALF), :] - slater * root)
        first, second = open0[...], open1[...]
        spread = [dot(high, first) + dot(low, first), dot(high, second) + dot(low, second)]
        value = [fields[pl.ds(pl.multiple_of((z * XB + i) * G, G), G), :] for i in range(XB)]
        product = jnp.concatenate(spread, axis=0) * jnp.concatenate(value, axis=1)
        out = transform(table, split(product))
        for i in range(XB):
            for y in range(GY):
                sent[pl.ds(y * COLS + z * XB + i, PW, stride=BLK), :] = out[
                    y * PW : (y + 1) * PW, i * LANES : (i + 1) * LANES
                ]
        return carry

    lax.fori_loop(0, GY, along_y, 0)


def spread_kernel(recv0, recv1, zt, mh, ml, dense, uv, bh, bl):
    table = zt[...]
    for p in range(2 * PAIRS):
        recv = (recv0, recv1)[p // PAIRS]
        starts = [y * COLS + z * XB + p % PAIRS * 2 for y in range(GY) for z in range(GY)]
        data = [lines(recv, [row + side for row in starts]) for side in range(2)]
        uv[p] = dot3(split(jnp.concatenate(data, axis=1)), (mh[p], ml[p]))

    def twelve(i, carry):
        at = pl.multiple_of(i * 16, 16)
        left = [uv[p, pl.ds(at, 16), :LANES] for p in range(6)]
        right = [uv[p, pl.ds(at, 16), LANES:] for p in range(6)]
        c, s = cos12(left + [right[0]]), sin12([None] + right[1:])
        x = [c[0]] + [c[j] + s[j] for j in range(1, 6)] + [c[6]] + [c[j] - s[j] for j in range(5, 0, -1)]
        for quad in range(3):
            high, low = split(jnp.concatenate(x[4 * quad : 4 * quad + 4], axis=1))
            bh[quad, pl.ds(at, 16), :] = high
            bl[quad, pl.ds(at, 16), :] = low
        return carry

    lax.fori_loop(0, GY * G // 16, twelve, 0)

    def along_z(i, carry):
        y, quad = i // 3, i % 3
        at = pl.multiple_of(y * G, G)
        out = transform(table, (bh[quad, pl.ds(at, G), :], bl[quad, pl.ds(at, G), :]))
        for side in range(4):
            base = (y * G + (quad * 4 + side) * 8) * G
            for r in range(0, G, 8):
                copies = spread_groups(out[r : r + 8, side * LANES : (side + 1) * LANES], (8, LANES))
                for xl in range(8):
                    dense[pl.ds(pl.multiple_of(base + xl * G + r, 8), 8), :] = copies[xl]
        return carry

    lax.fori_loop(0, GY * 3, along_z, 0)


def pick_kernel(cells, dense, *rest):
    terms, turned = rest[-1 - HELD : -1], rest[-1]
    masks = source_masks()

    def pick(i, carry):
        for j in range(16):
            k = i * 16 + j
            row = None
            for group in range(BD):
                half, p = group // HELD, group % HELD
                value = dense[pl.ds(cells[p * KW + half * FIRST + k], 1), :]
                row = value if row is None else jnp.where(masks[group], value, row)
            turned[pl.ds(k, 1), :] = row
        return carry

    lax.fori_loop(0, FIRST // 16, pick, 0)

    def turn(i, carry):
        at = pl.multiple_of(i * LANES, LANES)
        rows = turned[pl.ds(at, LANES), :].T
        for group in range(BD):
            half, p = group // HELD, group % HELD
            terms[p][:, pl.ds(half * FIRST + at, LANES)] = rows[group * LB : (group + 1) * LB]
        return carry

    lax.fori_loop(0, FIRST // LANES, turn, 0)


def rotate_kernel(order, weights, coefs, *rest):
    blocks, rotated = rest[-1 - BD : -1], rest[-1]
    turned = split(weights[...].T)
    for at in range(0, KW, 512):
        part = pl.ds(at, 512)
        rotated[:, part] = dot3(turned, split(coefs[:, part]))
    for p in range(BD):
        blocks[p][...] = rotated[pl.ds(pl.multiple_of(order[p] * LB, LB), LB), :]


def pullback_kernel(grads, s, y0, y1, y2, y3, z1, z2, z3, z4, t1, t2, t3, t4, coefs, first, out):
    def mul(a, b):
        return jnp.dot(a[...], b[...], precision=highest, preferred_element_type=f32)

    y, z, t = (y0, y1, y2, y3), (None, z1, z2, z3, z4), (None, t1, t2, t3, t4)
    values = s[...]
    squared = jnp.sum(values * values, keepdims=True)
    frob = jnp.sqrt(squared)
    root = jnp.sqrt(frob)
    given = grads[...]
    zb = given / root
    fb = -0.5 * jnp.sum(given * z4[...], keepdims=True) / (frob * root)
    yb = None
    for k in range(NS_ITERS, 0, -1):
        tb = zb if k == 1 else mul(zb, z[k - 1])
        if yb is not None:
            tb = tb + mul(y[k - 1], yb)
        before = tb if k == 1 else mul(z[k - 1], tb)
        before = -0.5 * before
        if yb is not None:
            before = before + mul(yb, t[k])
        if k > 1:
            zb = mul(t[k], zb) - 0.5 * mul(tb, y[k - 1])
        yb = before
    fb = fb - jnp.sum(yb * values, keepdims=True) / squared
    grad = yb / frob + fb * (values / frob)
    both = split((grad + grad.T) / NPW)
    for at in range(0, KW, 512):
        part = pl.ds(at, 512)
        out[:, part] = first[:, part] + dot3(both, split(coefs[:, part]))


def products_kernel(order, *rest):
    terms, rotated, (coefs, kinetic, occupancy, grads, sums) = rest[:BD], rest[BD : 2 * BD], rest[2 * BD :]
    for p in range(BD):
        rows = pl.ds(pl.multiple_of(order[p] * LB, LB), LB)
        grads[rows, :] = occupancy[rows, :] * (kinetic[...] * rotated[p][...] + terms[p][...])
    added = jnp.zeros((NB, NB), f32)

    def dot_t(a, b):
        return lax.dot_general(a, b, (((1,), (1,)), ((), ())), preferred_element_type=f32)

    for at in range(0, KW, 512):
        part = pl.ds(at, 512)
        a, b = split(coefs[:, part]), split(grads[:, part])
        added = added + (dot_t(a[0], b[0]) + (dot_t(a[0], b[1]) + dot_t(a[1], b[0])))
    sums[...] = added


def call(kernel, out_shapes, scratch, scalars, *operands, unread=(), alias=None, room=58, micros=3):
    vmem = pl.BlockSpec(memory_space=pltpu.VMEM)
    smem = pl.BlockSpec(memory_space=pltpu.SMEM)
    return pl.pallas_call(
        kernel,
        out_shape=out_shapes,
        in_specs=[smem] * scalars
        + [vmem] * (len(operands) - scalars)
        + [pl.BlockSpec(memory_space=pl.ANY)] * len(unread),
        out_specs=jax.tree.map(lambda _: vmem, out_shapes),
        scratch_shapes=scratch,
        input_output_aliases=alias or {},
        cost_estimate=pl.CostEstimate(flops=0, bytes_accessed=micros * 3_500_000, transcendentals=0),
        compiler_params=pltpu.CompilerParams(vmem_limit_bytes=room * 1024 * 1024),
    )(*operands, *unread)


def kept(*shape):
    return pltpu.VMEM(shape, f32)


def held(values):
    return pltpu.with_memory_space_constraint(values, pltpu.VMEM)


def array(*shape):
    return jax.ShapeDtypeStruct(shape, f32)


def matmul(left_side, right_side):
    return jnp.dot(left_side, right_side, precision=highest, preferred_element_type=f32)


def loewdin(intersection):
    frob_norm = jnp.sqrt(jnp.sum(intersection * intersection))
    identity = jnp.eye(intersection.shape[0], dtype=f32)
    ys, zs, ts = [intersection / frob_norm], [], []
    for repeat in range(NS_ITERS):
        product = matmul(zs[-1], ys[-1]) if zs else ys[-1]
        ts.append(1.5 * identity - 0.5 * product)
        zs.append(matmul(ts[-1], zs[-1]) if zs else ts[-1])
        if repeat < NS_ITERS - 1:
            ys.append(matmul(ys[-1], ts[-1]))
    return zs[-1] / jnp.sqrt(frob_norm), (*ys, *zs, *ts)


def total(values, beside=()):
    axes = ("pw", "band")
    pieces = lax.all_to_all(values, axes, split_axis=0, concat_axis=0, tiled=True)
    row = jnp.sum(pieces, axis=0, keepdims=True)
    row, *beside = lax.optimization_barrier((row, *beside))
    copies = jnp.broadcast_to(row, values.shape)
    return lax.all_to_all(copies, axes, split_axis=0, concat_axis=0, tiled=True), beside


def band_total(values):
    values = values + lax.ppermute(values, "band", [(i, i ^ 1) for i in range(BD)])
    others = [lax.ppermute(values, "band", [(i, (i + 2 * step) % BD) for i in range(BD)]) for step in (1, 2, 3)]
    return values + ((others[0] + others[2]) + others[1])


def packings():
    chosen = np.zeros((PARTS, 2, G, LANES))
    packed = np.zeros((PARTS, 2, WIDE, LANES))
    for part in range(PARTS):
        blocks = [m for pair in BLOCKS[part * PAIRS : (part + 1) * PAIRS] for m in pair]
        for half in range(2):
            for i, m in enumerate(blocks):
                for q in range(BD):
                    lane = half * 64 + i * BD + q
                    chosen[part, half, m + 12 * q, lane] = 1
                    row = i * LANES + q * LB
                    packed[part, half, row : row + LB, lane] = 1
    return chosen, packed


def to_sums(planes, chosen):
    values = planes.reshape(GY, 2, HALF, G)
    packed = matmul(values[:, 0], chosen[0]) + matmul(values[:, 1], chosen[1])
    return packed.reshape(SUM_ROWS, LANES)


def from_sums(parts, chosen):
    halves_of_y = [
        sum(matmul(parts[part], chosen[part, half].T) for part in range(PARTS)).reshape(GY, 1, HALF, G)
        for half in range(2)
    ]
    return jnp.concatenate(halves_of_y, axis=1).reshape(GY, G * G)


def shards(coefficients, occupancy, kinetic, cell_map, potential_ext, core_density):
    table = tables()
    chosen, packed = packings()
    chosen = chosen.astype(np.float32)
    pack = packed[0].astype(ml_dtypes.bfloat16)
    unpack = np.swapaxes(pack, 1, 2)
    unused_lanes = (1.0 - chosen.sum(axis=(1, 2))).astype(np.float32)
    pw_pos = lax.axis_index("pw")
    band_pos = lax.axis_index("band")
    cells = cell_map - pw_pos * SLAB

    order = jnp.bitwise_xor(band_pos, jnp.asarray(ORDER, jnp.int32))
    cells = [lax.dynamic_slice_in_dim(cells, order[p] * KW, KW) for p in range(BD)]
    cells = [jnp.concatenate(cells[:HELD]), jnp.concatenate(cells[HELD:])]

    def meet(block, p):
        if ORDER[p] == 0:
            return block
        return lax.ppermute(block, "band", [(i, i ^ ORDER[p]) for i in range(BD)])

    intersection, planes = total(matmul(coefficients, coefficients.T), (core_density, potential_ext))
    intersection = intersection / NPW
    core = [to_sums(planes[0], chosen[part]) + unused_lanes[part] for part in range(PARTS)]
    external = [to_sums(planes[1], chosen[part]) for part in range(PARTS)]
    weights, iterates = loewdin(intersection)
    rotated = call(
        rotate_kernel,
        [array(LB, KW)] * BD,
        [pltpu.VMEM((NB, KW), f32)],
        1,
        order,
        weights,
        coefficients,
        unread=(*cells, *core, *external),
        room=28,
    )
    near = [meet(rotated[p], p) for p in range(HELD)]
    dense = call(clear_kernel, kept(SLAB, LANES), [], 0, unread=(rotated[0],), room=28)
    *barred, dense = lax.optimization_barrier((*near, *rotated[HELD:], dense))
    blocks = [*barred[:HELD], *(meet(barred[p], p) for p in range(HELD, BD))]
    dense = call(
        place_kernel,
        kept(SLAB, LANES),
        [pltpu.VMEM((FIRST, LANES), f32)],
        1,
        cells[0],
        *blocks[:HELD],
        held(dense),
        alias={1 + HELD: 0},
        room=28,
        micros=14,
    )
    halves_shape = (2 * PAIRS, GY * G, 2 * LANES)
    unused, *sent = call(
        fold_kernel,
        (kept(SLAB, LANES), array(ROWS, LANES), array(ROWS, LANES)),
        [
            pltpu.VMEM((FIRST, LANES), f32),
            pltpu.VMEM((12, GY * G, LANES), f32),
            pltpu.VMEM(halves_shape, bf16),
            pltpu.VMEM(halves_shape, bf16),
        ],
        1,
        cells[1],
        *blocks[HELD:],
        held(dense),
        table["z_out"],
        *table["mix"],
        alias={1 + HELD: 0},
        room=28,
        micros=29,
    )
    *sent, kinetic, occupancy = lax.optimization_barrier((*sent, kinetic, occupancy))
    share = lax.dynamic_slice_in_dim(occupancy / NB, band_pos * LB, LB)
    share = jnp.tile(share, XB * BD).reshape(1, WIDE)
    kinetic_row = kinetic.reshape(1, KW)
    occupancy_column = occupancy.reshape(NB, 1)
    exchange = functools.partial(lax.all_to_all, axis_name="pw", split_axis=0, concat_axis=0, tiled=True)
    density, returned, after = [], [], []
    for part in range(PARTS):
        received = exchange(sent[part])
        fields, sums = call(
            density_kernel,
            (array(ROWS, LANES), array(SUM_ROWS, LANES)),
            [],
            0,
            received,
            table["y_out"],
            *pack,
            share,
            unread=after,
        )
        density.append(core[part] + band_total(sums))
        product = call(
            potential_kernel,
            array(ROWS, LANES),
            [],
            0,
            density[part],
            external[part],
            fields,
            table["y_in"],
            *unpack,
        )
        after = [product]
        returned.append(exchange(product))
    dense = call(
        spread_kernel,
        kept(SLAB, LANES),
        [
            pltpu.VMEM((6, GY * G, 2 * LANES), f32),
            pltpu.VMEM((3, GY * G, 4 * LANES), bf16),
            pltpu.VMEM((3, GY * G, 4 * LANES), bf16),
        ],
        0,
        *returned,
        table["z_in"],
        *table["mix_t"],
        room=28,
        micros=13,
    )
    terms, after = [None, None], ()
    for side in (1, 0):
        terms[side] = call(
            pick_kernel,
            [array(LB, KW)] * HELD,
            [pltpu.VMEM((FIRST, LANES), f32)],
            1,
            cells[side],
            held(dense),
            unread=after,
            room=28,
            micros=14,
        )
        after = tuple(terms[side])
    far = [meet(terms[1][p], HELD + p) for p in range(HELD)]
    near = terms[0]
    barred = lax.optimization_barrier((*near, *far))
    near, far = barred[:HELD], barred[HELD:]
    terms = [meet(near[p], p) for p in range(HELD)] + list(far)
    grad_rotated, partial = call(
        products_kernel,
        (array(NB, KW), array(NB, NB)),
        [],
        1,
        order,
        *terms,
        *rotated,
        coefficients,
        kinetic_row,
        occupancy_column,
    )
    *density, partial = lax.optimization_barrier((*density, partial))
    grad_weights, unneeded = total(partial)
    first = matmul(weights, grad_rotated)
    grad_coef = call(
        pullback_kernel, array(NB, KW), [], 0, grad_weights, intersection, *iterates, coefficients, first
    )
    return (grad_coef, from_sums(density, chosen))


def solution(mesh):
    placed = (
        P(None, ("pw", "band")),
        P(),
        P(("pw", "band")),
        P("pw"),
        P("pw", None),
        P("pw", None),
    )
    return jax.shard_map(
        shards,
        mesh=mesh,
        in_specs=placed,
        out_specs=(P(None, ("pw", "band")), P("pw", None)),
        check_vma=False,
    )
```

```python
import functools
import math

import jax
import jax.numpy as jnp
import ml_dtypes
import numpy as np
from jax import lax
from jax.experimental import pallas as pl
from jax.experimental.pallas import tpu as pltpu
from jax.sharding import PartitionSpec as P

G = 96
NPW = 393216
NB = 128
NS_ITERS = 4
PW = 16
BD = 8
LB = NB // BD
GY = G // PW
ORDER = (0, 1, 2, 6, 3, 7, 4, 5)
HELD = BD // 2
FIRST = NPW // (PW * BD) // 2
PARTS = 2
BLOCKS = ((0, 6), (1, 11), (2, 10), (3, 9), (4, 8), (5, 7))
PAIRS = len(BLOCKS) // PARTS
XB = 2 * PAIRS
COLS = GY * XB
HALF = G // 2
WIDE = XB * 128
SLAB = GY * G * G
KW = NPW // (PW * BD)
BLK = GY * COLS
ROWS = PW * BLK
SUM_ROWS = GY * HALF
LANES = 128

highest = lax.Precision.HIGHEST
slater = 0.9847450218426965
bf16 = jnp.bfloat16
f32 = jnp.float32


def halves(table):
    high = table.astype(ml_dtypes.bfloat16)
    low = (table - high.astype(np.float64)).astype(ml_dtypes.bfloat16)
    return high, low


def tables():
    counter = np.arange(G)
    phases = 2.0 * np.pi / G * (counter[:, None] * counter[None, :] % G)
    cas = np.cos(phases) + np.sin(phases)
    order = (np.arange(PW)[None, :] * GY + np.arange(GY)[:, None]).reshape(-1)
    scaled = cas / math.sqrt(NPW)
    mixes = []
    small = np.arange(8)

    def mix(m):
        beta = 2.0 * np.pi / G * (small[:, None] * (m + 12 * small[None, :]))
        even = np.kron(np.cos(beta) + np.sin(beta), np.eye(LB))
        odd = np.kron(np.cos(beta) - np.sin(beta), np.eye(LB))
        return even, odd

    zero = np.zeros((LANES, LANES))
    mixes.append(np.block([[mix(0)[0], zero], [zero, mix(6)[0]]]))
    for m in range(1, 6):
        here, there = mix(m), mix(12 - m)
        mixes.append(np.block([[here[0], there[0]], [here[1], -there[1]]]))
    mixes = np.stack(mixes)
    return dict(
        z_out=np.concatenate(halves(scaled[order, :])),
        y_out=np.concatenate(halves(cas[:, order])),
        y_in=np.concatenate(halves(cas[order, :])),
        z_in=np.concatenate(halves(scaled[:, order])),
        mix=halves(mixes),
        mix_t=halves(np.swapaxes(mixes, 1, 2)),
    )


ROOT3 = math.sqrt(3.0) / 2.0


def cos12(e):
    a0, a1, a2 = e[0] + e[6], e[1] + e[5], e[2] + e[4]
    b0, b1, b2 = e[0] - e[6], e[1] - e[5], e[2] - e[4]
    t = ROOT3 * b1
    h = b0 + 0.5 * b2
    r = 0.5 * (a1 + a2)
    d = 0.5 * (a1 - a2)
    return [
        a0 + a1 + a2 + e[3],
        h + t,
        a0 + d - e[3],
        b0 - b2,
        a0 - r + e[3],
        h - t,
        a0 - a1 + a2 - e[3],
    ]


def sin12(o):
    p1, p2 = o[1] + o[5], o[2] + o[4]
    r1, r2 = o[1] - o[5], o[2] - o[4]
    h = 0.5 * p1 + o[3]
    t = ROOT3 * p2
    return [None, h + t, ROOT3 * (r1 + r2), p1 - o[3], ROOT3 * (r1 - r2), h - t]


def split(values):
    high = values.astype(bf16)
    return high, (values - high.astype(f32)).astype(bf16)


def dot(a, b):
    return jnp.dot(a, b, preferred_element_type=f32)


def dot3(a, b):
    return dot(a[0], b[0]) + (dot(a[0], b[1]) + dot(a[1], b[0]))


def transform(table, b):
    rows = table.shape[0] // 2
    both = dot(table, b[0])
    return both[:rows] + (dot(table[:rows], b[1]) + both[rows:])


def lane_bit(shape, bit):
    return (lax.broadcasted_iota(jnp.int32, shape, 1) & bit) == 0


def gather_groups(parts, shape):
    for width in (16, 32, 64):
        first = lane_bit(shape, width)
        parts = [
            jnp.where(first, a, b) + pltpu.roll(jnp.where(first, b, a), width, 1)
            for a, b in zip(parts[0::2], parts[1::2])
        ]
    return parts[0]


def spread_groups(value, shape):
    parts = [value]
    for width in (64, 32, 16):
        first = lane_bit(shape, width)
        turned = [pltpu.roll(part, width, 1) for part in parts]
        parts = [
            side
            for part, turn in zip(parts, turned)
            for side in (jnp.where(first, part, turn), jnp.where(first, turn, part))
        ]
    return parts


def lines(ref, start):
    return jnp.concatenate([ref[pl.ds(row, PW, stride=BLK), :] for row in start], axis=0)


def source_masks():
    group = lax.broadcasted_iota(jnp.int32, (1, LANES), 1) // LB
    return [group == s for s in range(BD)]


def clear_kernel(unread, dense):
    zero = jnp.zeros((256, LANES), f32)

    def clear(i, carry):
        dense[pl.ds(pl.multiple_of(i * 256, 256), 256), :] = zero
        return carry

    lax.fori_loop(0, SLAB // 256, clear, 0)


def place_kernel(cells, *rest):
    blocks, (dense, turned) = rest[:HELD], rest[-2:]

    def turn(i, carry):
        at = pl.multiple_of(i * LANES, LANES)
        rows = [block[:, pl.ds(half * FIRST + at, LANES)] for half in range(2) for block in blocks]
        turned[pl.ds(at, LANES), :] = jnp.concatenate(rows, axis=0).T
        return carry

    lax.fori_loop(0, FIRST // LANES, turn, 0)
    masks = source_masks()

    def place(i, carry):
        for j in range(16):
            k = i * 16 + j
            row = turned[pl.ds(k, 1), :]
            for group in range(BD):
                half, p = group // HELD, group % HELD
                cell = cells[p * KW + half * FIRST + k]
                pltpu.store(dense.at[pl.ds(cell, 1), :], row, mask=masks[group])
        return carry

    lax.fori_loop(0, FIRST // 16, place, 0)


def fold_kernel(cells, *rest):
    given, zt, mh, ml, dense, sent0, sent1, turned, fields, high, low = rest[HELD:]
    place_kernel(cells, *rest[:HELD], dense, turned)
    table = zt[...]

    def along_z(i, carry):
        y, quad = i // 3, i % 3
        folded = []
        for side in range(4):
            base = (y * G + (quad * 4 + side) * 8) * G
            tiles = []
            for r in range(0, G, 8):
                parts = [dense[pl.ds(pl.multiple_of(base + xl * G + r, 8), 8), :] for xl in range(8)]
                tiles.append(gather_groups(parts, (8, LANES)))
            folded.append(jnp.concatenate(tiles, axis=0))
        out = transform(table, split(jnp.concatenate(folded, axis=1)))
        at = pl.multiple_of(y * G, G)
        for side in range(4):
            fields[quad * 4 + side, pl.ds(at, G), :] = out[:, side * LANES : (side + 1) * LANES]
        return carry

    lax.fori_loop(0, GY * 3, along_z, 0)

    def twelve(i, carry):
        at = pl.multiple_of(i * 16, 16)
        e = [fields[xh, pl.ds(at, 16), :] for xh in range(12)]
        c = cos12([e[0]] + [e[j] + e[12 - j] for j in range(1, 6)] + [e[6]])
        s = sin12([None] + [e[j] - e[12 - j] for j in range(1, 6)])
        for p in range(6):
            high[p, pl.ds(at, 16), :], low[p, pl.ds(at, 16), :] = split(
                jnp.concatenate([c[p], c[6] if p == 0 else s[p]], axis=1)
            )
        return carry

    lax.fori_loop(0, GY * G // 16, twelve, 0)
    for p in range(2 * PAIRS):
        out = dot3((high[p], low[p]), (mh[p], ml[p]))
        sent = (sent0, sent1)[p // PAIRS]
        for side in range(2):
            for y in range(GY):
                for z in range(GY):
                    at = y * G + z * PW
                    sent[pl.ds(y * COLS + z * XB + p % PAIRS * 2 + side, PW, stride=BLK), :] = out[
                        at : at + PW, side * LANES : (side + 1) * LANES
                    ]


def lane_of(shape, dim, half):
    wide = lax.broadcasted_iota(jnp.int32, shape, dim) // LB
    lane = lax.broadcasted_iota(jnp.int32, shape, 1 - dim)
    return jnp.where(wide + 64 * half == lane, 1.0, 0.0).astype(bf16)


def density_kernel(recv, yt, share, *rest):
    fields, sums = rest[-2:]
    table = yt[...]
    weight = share[...]
    first, second = [lane_of((WIDE, LANES), 0, half) for half in range(2)]

    def along_y(z, carry):
        data = [lines(recv, [y * COLS + z * XB + i for y in range(GY)]) for i in range(XB)]
        out = transform(table, split(jnp.concatenate(data, axis=1)))
        for i in range(XB):
            at = pl.multiple_of((z * XB + i) * G, G)
            fields[pl.ds(at, G), :] = out[:, i * LANES : (i + 1) * LANES]
        high, low = split(weight * out * out)
        added = dot(high[:HALF], first) + dot(low[:HALF], first)
        added = added + (dot(high[HALF:], second) + dot(low[HALF:], second))
        sums[pl.ds(pl.multiple_of(z * HALF, HALF), HALF), :] = added
        return carry

    lax.fori_loop(0, GY, along_y, 0)


def potential_kernel(density, external, fields, yt, sent):
    table = yt[...]
    first, second = [lane_of((LANES, WIDE), 1, half) for half in range(2)]

    def along_y(z, carry):
        at = pl.multiple_of(z * HALF, HALF)
        dens = density[pl.ds(at, HALF), :]
        root = jnp.exp(jnp.log(dens) * (1.0 / 3.0))
        root = root - (root - dens / (root * root)) * (1.0 / 3.0)
        high, low = split(external[pl.ds(at, HALF), :] - slater * root)
        spread = [dot(high, first) + dot(low, first), dot(high, second) + dot(low, second)]
        value = [fields[pl.ds(pl.multiple_of((z * XB + i) * G, G), G), :] for i in range(XB)]
        product = jnp.concatenate(spread, axis=0) * jnp.concatenate(value, axis=1)
        out = transform(table, split(product))
        for i in range(XB):
            for y in range(GY):
                sent[pl.ds(y * COLS + z * XB + i, PW, stride=BLK), :] = out[
                    y * PW : (y + 1) * PW, i * LANES : (i + 1) * LANES
                ]
        return carry

    lax.fori_loop(0, GY, along_y, 0)


def spread_kernel(recv0, recv1, zt, mh, ml, dense, uv, bh, bl):
    table = zt[...]
    for p in range(2 * PAIRS):
        recv = (recv0, recv1)[p // PAIRS]
        starts = [y * COLS + z * XB + p % PAIRS * 2 for y in range(GY) for z in range(GY)]
        data = [lines(recv, [row + side for row in starts]) for side in range(2)]
        uv[p] = dot3(split(jnp.concatenate(data, axis=1)), (mh[p], ml[p]))

    def twelve(i, carry):
        at = pl.multiple_of(i * 16, 16)
        left = [uv[p, pl.ds(at, 16), :LANES] for p in range(6)]
        right = [uv[p, pl.ds(at, 16), LANES:] for p in range(6)]
        c, s = cos12(left + [right[0]]), sin12([None] + right[1:])
        x = [c[0]] + [c[j] + s[j] for j in range(1, 6)] + [c[6]] + [c[j] - s[j] for j in range(5, 0, -1)]
        for quad in range(3):
            high, low = split(jnp.concatenate(x[4 * quad : 4 * quad + 4], axis=1))
            bh[quad, pl.ds(at, 16), :] = high
            bl[quad, pl.ds(at, 16), :] = low
        return carry

    lax.fori_loop(0, GY * G // 16, twelve, 0)

    def along_z(i, carry):
        y, quad = i // 3, i % 3
        at = pl.multiple_of(y * G, G)
        out = transform(table, (bh[quad, pl.ds(at, G), :], bl[quad, pl.ds(at, G), :]))
        for side in range(4):
            base = (y * G + (quad * 4 + side) * 8) * G
            for r in range(0, G, 8):
                copies = spread_groups(out[r : r + 8, side * LANES : (side + 1) * LANES], (8, LANES))
                for xl in range(8):
                    dense[pl.ds(pl.multiple_of(base + xl * G + r, 8), 8), :] = copies[xl]
        return carry

    lax.fori_loop(0, GY * 3, along_z, 0)


def pick_kernel(cells, dense, *rest):
    terms, turned = rest[-1 - HELD : -1], rest[-1]
    masks = source_masks()

    def pick(i, carry):
        for j in range(16):
            k = i * 16 + j
            row = None
            for group in range(BD):
                half, p = group // HELD, group % HELD
                value = dense[pl.ds(cells[p * KW + half * FIRST + k], 1), :]
                row = value if row is None else jnp.where(masks[group], value, row)
            turned[pl.ds(k, 1), :] = row
        return carry

    lax.fori_loop(0, FIRST // 16, pick, 0)

    def turn(i, carry):
        at = pl.multiple_of(i * LANES, LANES)
        rows = turned[pl.ds(at, LANES), :].T
        for group in range(BD):
            half, p = group // HELD, group % HELD
            terms[p][:, pl.ds(half * FIRST + at, LANES)] = rows[group * LB : (group + 1) * LB]
        return carry

    lax.fori_loop(0, FIRST // LANES, turn, 0)


def rotate_kernel(order, weights, coefs, *rest):
    blocks, rotated = rest[-1 - BD : -1], rest[-1]
    turned = split(weights[...].T)
    for at in range(0, KW, 512):
        part = pl.ds(at, 512)
        rotated[:, part] = dot3(turned, split(coefs[:, part]))
    for p in range(BD):
        blocks[p][...] = rotated[pl.ds(pl.multiple_of(order[p] * LB, LB), LB), :]


def pullback_kernel(grads, s, y0, y1, y2, y3, z1, z2, z3, z4, t1, t2, t3, t4, coefs, first, out):
    def mul(a, b):
        return jnp.dot(a[...], b[...], precision=highest, preferred_element_type=f32)

    y, z, t = (y0, y1, y2, y3), (None, z1, z2, z3, z4), (None, t1, t2, t3, t4)
    values = s[...]
    squared = jnp.sum(values * values, keepdims=True)
    frob = jnp.sqrt(squared)
    root = jnp.sqrt(frob)
    given = grads[...]
    zb = given / root
    fb = -0.5 * jnp.sum(given * z4[...], keepdims=True) / (frob * root)
    yb = None
    for k in range(NS_ITERS, 0, -1):
        tb = zb if k == 1 else mul(zb, z[k - 1])
        if yb is not None:
            tb = tb + mul(y[k - 1], yb)
        before = tb if k == 1 else mul(z[k - 1], tb)
        before = -0.5 * before
        if yb is not None:
            before = before + mul(yb, t[k])
        if k > 1:
            zb = mul(t[k], zb) - 0.5 * mul(tb, y[k - 1])
        yb = before
    fb = fb - jnp.sum(yb * values, keepdims=True) / squared
    grad = yb / frob + fb * (values / frob)
    both = split((grad + grad.T) / NPW)
    for at in range(0, KW, 512):
        part = pl.ds(at, 512)
        out[:, part] = first[:, part] + dot3(both, split(coefs[:, part]))


def dot_t(a, b):
    return lax.dot_general(a, b, (((1,), (1,)), ((), ())), preferred_element_type=f32)


def gram_kernel(coefs, out):
    equal = jnp.zeros((NB, NB), f32)
    mixed = jnp.zeros((NB, NB), f32)
    for at in range(0, KW, 512):
        high, low = split(coefs[:, pl.ds(at, 512)])
        equal = equal + dot_t(high, high)
        mixed = mixed + dot_t(high, low)
    out[...] = equal + (mixed + mixed.T)


def products_kernel(order, *rest):
    terms, rotated, (coefs, kinetic, occupancy, grads, sums) = rest[:BD], rest[BD : 2 * BD], rest[2 * BD :]
    for p in range(BD):
        rows = pl.ds(pl.multiple_of(order[p] * LB, LB), LB)
        grads[rows, :] = occupancy[rows, :] * (kinetic[...] * rotated[p][...] + terms[p][...])
    added = jnp.zeros((NB, NB), f32)
    for at in range(0, KW, 512):
        part = pl.ds(at, 512)
        a, b = split(coefs[:, part]), split(grads[:, part])
        added = added + (dot_t(a[0], b[0]) + (dot_t(a[0], b[1]) + dot_t(a[1], b[0])))
    sums[...] = added


def call(kernel, out_shapes, scratch, scalars, *operands, unread=(), alias=None, room=58, micros=3):
    vmem = pl.BlockSpec(memory_space=pltpu.VMEM)
    smem = pl.BlockSpec(memory_space=pltpu.SMEM)
    return pl.pallas_call(
        kernel,
        out_shape=out_shapes,
        in_specs=[smem] * scalars
        + [vmem] * (len(operands) - scalars)
        + [pl.BlockSpec(memory_space=pl.ANY)] * len(unread),
        out_specs=jax.tree.map(lambda _: vmem, out_shapes),
        scratch_shapes=scratch,
        input_output_aliases=alias or {},
        cost_estimate=pl.CostEstimate(flops=0, bytes_accessed=micros * 3_500_000, transcendentals=0),
        compiler_params=pltpu.CompilerParams(vmem_limit_bytes=room * 1024 * 1024),
    )(*operands, *unread)


def kept(*shape):
    return pltpu.VMEM(shape, f32)


def held(values):
    return pltpu.with_memory_space_constraint(values, pltpu.VMEM)


def array(*shape):
    return jax.ShapeDtypeStruct(shape, f32)


def matmul(left_side, right_side):
    return jnp.dot(left_side, right_side, precision=highest, preferred_element_type=f32)


def loewdin(intersection):
    frob_norm = jnp.sqrt(jnp.sum(intersection * intersection))
    identity = jnp.eye(intersection.shape[0], dtype=f32)
    ys, zs, ts = [intersection / frob_norm], [], []
    for repeat in range(NS_ITERS):
        product = matmul(zs[-1], ys[-1]) if zs else ys[-1]
        ts.append(1.5 * identity - 0.5 * product)
        zs.append(matmul(ts[-1], zs[-1]) if zs else ts[-1])
        if repeat < NS_ITERS - 1:
            ys.append(matmul(ys[-1], ts[-1]))
    return zs[-1] / jnp.sqrt(frob_norm), (*ys, *zs, *ts)


def total(values, beside=()):
    axes = ("pw", "band")
    pieces = lax.all_to_all(values, axes, split_axis=0, concat_axis=0, tiled=True)
    row = jnp.sum(pieces, axis=0, keepdims=True)
    row, *beside = lax.optimization_barrier((row, *beside))
    copies = jnp.broadcast_to(row, values.shape)
    return lax.all_to_all(copies, axes, split_axis=0, concat_axis=0, tiled=True), beside


def band_total(values):
    values = values + lax.ppermute(values, "band", [(i, i ^ 1) for i in range(BD)])
    others = [lax.ppermute(values, "band", [(i, (i + 2 * step) % BD) for i in range(BD)]) for step in (1, 2, 3)]
    return values + ((others[0] + others[2]) + others[1])


def packings():
    chosen = np.zeros((PARTS, 2, G, LANES), np.float32)
    for part in range(PARTS):
        blocks = [m for pair in BLOCKS[part * PAIRS : (part + 1) * PAIRS] for m in pair]
        for half in range(2):
            for i, m in enumerate(blocks):
                for q in range(BD):
                    chosen[part, half, m + 12 * q, half * 64 + i * BD + q] = 1
    return chosen


def to_sums(planes, chosen):
    values = planes.reshape(GY, 2, HALF, G)
    packed = matmul(values[:, 0], chosen[0]) + matmul(values[:, 1], chosen[1])
    return packed.reshape(SUM_ROWS, LANES)


def from_sums(parts, chosen):
    halves_of_y = [
        sum(matmul(parts[part], chosen[part, half].T) for part in range(PARTS)).reshape(GY, 1, HALF, G)
        for half in range(2)
    ]
    return jnp.concatenate(halves_of_y, axis=1).reshape(GY, G * G)


def shards(coefficients, occupancy, kinetic, cell_map, potential_ext, core_density):
    table = tables()
    chosen = packings()
    unused_lanes = (1.0 - chosen.sum(axis=(1, 2))).astype(np.float32)
    pw_pos = lax.axis_index("pw")
    band_pos = lax.axis_index("band")
    cells = cell_map - pw_pos * SLAB

    order = jnp.bitwise_xor(band_pos, jnp.asarray(ORDER, jnp.int32))
    cells = [lax.dynamic_slice_in_dim(cells, order[p] * KW, KW) for p in range(BD)]
    cells = [jnp.concatenate(cells[:HELD]), jnp.concatenate(cells[HELD:])]

    def meet(block, p):
        if ORDER[p] == 0:
            return block
        return lax.ppermute(block, "band", [(i, i ^ ORDER[p]) for i in range(BD)])

    intersection, planes = total(call(gram_kernel, array(NB, NB), [], 0, coefficients), (core_density, potential_ext))
    intersection = intersection / NPW
    core = [to_sums(planes[0], chosen[part]) + unused_lanes[part] for part in range(PARTS)]
    external = [to_sums(planes[1], chosen[part]) for part in range(PARTS)]
    weights, iterates = loewdin(intersection)
    rotated = call(
        rotate_kernel,
        [array(LB, KW)] * BD,
        [pltpu.VMEM((NB, KW), f32)],
        1,
        order,
        weights,
        coefficients,
        unread=(*cells, *core, *external),
        room=28,
    )
    near = [meet(rotated[p], p) for p in range(HELD)]
    dense = call(clear_kernel, kept(SLAB, LANES), [], 0, unread=(rotated[0],), room=28)
    *barred, dense = lax.optimization_barrier((*near, *rotated[HELD:], dense))
    blocks = [*barred[:HELD], *(meet(barred[p], p) for p in range(HELD, BD))]
    dense = call(
        place_kernel,
        kept(SLAB, LANES),
        [pltpu.VMEM((FIRST, LANES), f32)],
        1,
        cells[0],
        *blocks[:HELD],
        held(dense),
        alias={1 + HELD: 0},
        room=28,
        micros=14,
    )
    halves_shape = (2 * PAIRS, GY * G, 2 * LANES)
    unused, *sent = call(
        fold_kernel,
        (kept(SLAB, LANES), array(ROWS, LANES), array(ROWS, LANES)),
        [
            pltpu.VMEM((FIRST, LANES), f32),
            pltpu.VMEM((12, GY * G, LANES), f32),
            pltpu.VMEM(halves_shape, bf16),
            pltpu.VMEM(halves_shape, bf16),
        ],
        1,
        cells[1],
        *blocks[HELD:],
        held(dense),
        table["z_out"],
        *table["mix"],
        alias={1 + HELD: 0},
        room=28,
        micros=29,
    )
    *sent, kinetic, occupancy = lax.optimization_barrier((*sent, kinetic, occupancy))
    share = lax.dynamic_slice_in_dim(occupancy / NB, band_pos * LB, LB)
    share = jnp.tile(share, XB * BD).reshape(1, WIDE)
    kinetic_row = kinetic.reshape(1, KW)
    occupancy_column = occupancy.reshape(NB, 1)
    exchange = functools.partial(lax.all_to_all, axis_name="pw", split_axis=0, concat_axis=0, tiled=True)
    density, returned, after = [], [], []
    for part in range(PARTS):
        received = exchange(sent[part])
        fields, sums = call(
            density_kernel,
            (array(ROWS, LANES), array(SUM_ROWS, LANES)),
            [],
            0,
            received,
            table["y_out"],
            share,
            unread=after,
            room=28,
            micros=6,
        )
        density.append(core[part] + band_total(sums))
        product = call(
            potential_kernel,
            array(ROWS, LANES),
            [],
            0,
            density[part],
            external[part],
            fields,
            table["y_in"],
            room=28,
            micros=6,
        )
        after = [product]
        returned.append(exchange(product))
    dense = call(
        spread_kernel,
        kept(SLAB, LANES),
        [
            pltpu.VMEM((6, GY * G, 2 * LANES), f32),
            pltpu.VMEM((3, GY * G, 4 * LANES), bf16),
            pltpu.VMEM((3, GY * G, 4 * LANES), bf16),
        ],
        0,
        *returned,
        table["z_in"],
        *table["mix_t"],
        room=28,
        micros=13,
    )
    terms, after = [None, None], ()
    for side in (1, 0):
        terms[side] = call(
            pick_kernel,
            [array(LB, KW)] * HELD,
            [pltpu.VMEM((FIRST, LANES), f32)],
            1,
            cells[side],
            held(dense),
            unread=after,
            room=28,
            micros=14,
        )
        after = tuple(terms[side])
    far = [meet(terms[1][p], HELD + p) for p in range(HELD)]
    near = terms[0]
    barred = lax.optimization_barrier((*near, *far))
    near, far = barred[:HELD], barred[HELD:]
    terms = [meet(near[p], p) for p in range(HELD)] + list(far)
    grad_rotated, partial = call(
        products_kernel,
        (array(NB, KW), array(NB, NB)),
        [],
        1,
        order,
        *terms,
        *rotated,
        coefficients,
        kinetic_row,
        occupancy_column,
    )
    *density, partial = lax.optimization_barrier((*density, partial))
    grad_weights, unneeded = total(partial)
    first = matmul(weights, grad_rotated)
    grad_coef = call(
        pullback_kernel, array(NB, KW), [], 0, grad_weights, intersection, *iterates, coefficients, first
    )
    return (grad_coef, from_sums(density, chosen))


def solution(mesh):
    placed = (
        P(None, ("pw", "band")),
        P(),
        P(("pw", "band")),
        P("pw"),
        P("pw", None),
        P("pw", None),
    )
    return jax.shard_map(
        shards,
        mesh=mesh,
        in_specs=placed,
        out_specs=(P(None, ("pw", "band")), P("pw", None)),
        check_vma=False,
    )
```

```python
import functools
import math

import jax
import jax.numpy as jnp
import ml_dtypes
import numpy as np
from jax import lax
from jax.experimental import pallas as pl
from jax.experimental.pallas import tpu as pltpu
from jax.sharding import PartitionSpec as P

G = 96
NPW = 393216
NB = 128
NS_ITERS = 4
PW = 16
BD = 8
LB = NB // BD
GY = G // PW
ORDER = (0, 1, 2, 6, 3, 7, 4, 5)
HELD = BD // 2
FIRST = NPW // (PW * BD) // 2
PARTS = 2
BLOCKS = ((0, 6), (1, 11), (2, 10), (3, 9), (4, 8), (5, 7))
PAIRS = len(BLOCKS) // PARTS
XB = 2 * PAIRS
COLS = GY * XB
HALF = G // 2
WIDE = XB * 128
SLAB = GY * G * G
KW = NPW // (PW * BD)
BLK = GY * COLS
ROWS = PW * BLK
SUM_ROWS = GY * HALF
LANES = 128

highest = lax.Precision.HIGHEST
slater = 0.9847450218426965
bf16 = jnp.bfloat16
f32 = jnp.float32


def halves(table):
    high = table.astype(ml_dtypes.bfloat16)
    low = (table - high.astype(np.float64)).astype(ml_dtypes.bfloat16)
    return high, low


def tables():
    counter = np.arange(G)
    phases = 2.0 * np.pi / G * (counter[:, None] * counter[None, :] % G)
    cas = np.cos(phases) + np.sin(phases)
    order = (np.arange(PW)[None, :] * GY + np.arange(GY)[:, None]).reshape(-1)
    scaled = cas / math.sqrt(NPW)
    mixes = []
    small = np.arange(8)

    def mix(m):
        beta = 2.0 * np.pi / G * (small[:, None] * (m + 12 * small[None, :]))
        even = np.kron(np.cos(beta) + np.sin(beta), np.eye(LB))
        odd = np.kron(np.cos(beta) - np.sin(beta), np.eye(LB))
        return even, odd

    zero = np.zeros((LANES, LANES))
    mixes.append(np.block([[mix(0)[0], zero], [zero, mix(6)[0]]]))
    for m in range(1, 6):
        here, there = mix(m), mix(12 - m)
        mixes.append(np.block([[here[0], there[0]], [here[1], -there[1]]]))
    mixes = np.stack(mixes)
    return dict(
        z_out=np.concatenate(halves(scaled[order, :])),
        y_out=np.concatenate(halves(cas[:, order])),
        y_in=np.concatenate(halves(cas[order, :])),
        z_in=np.concatenate(halves(scaled[:, order])),
        mix=halves(mixes),
        mix_t=halves(np.swapaxes(mixes, 1, 2)),
    )


ROOT3 = math.sqrt(3.0) / 2.0


def cos12(e):
    a0, a1, a2 = e[0] + e[6], e[1] + e[5], e[2] + e[4]
    b0, b1, b2 = e[0] - e[6], e[1] - e[5], e[2] - e[4]
    t = ROOT3 * b1
    h = b0 + 0.5 * b2
    r = 0.5 * (a1 + a2)
    d = 0.5 * (a1 - a2)
    return [
        a0 + a1 + a2 + e[3],
        h + t,
        a0 + d - e[3],
        b0 - b2,
        a0 - r + e[3],
        h - t,
        a0 - a1 + a2 - e[3],
    ]


def sin12(o):
    p1, p2 = o[1] + o[5], o[2] + o[4]
    r1, r2 = o[1] - o[5], o[2] - o[4]
    h = 0.5 * p1 + o[3]
    t = ROOT3 * p2
    return [None, h + t, ROOT3 * (r1 + r2), p1 - o[3], ROOT3 * (r1 - r2), h - t]


def split(values):
    high = values.astype(bf16)
    return high, (values - high.astype(f32)).astype(bf16)


def dot(a, b):
    return jnp.dot(a, b, preferred_element_type=f32)


def dot3(a, b):
    return dot(a[0], b[0]) + (dot(a[0], b[1]) + dot(a[1], b[0]))


def transform(table, b):
    rows = table.shape[0] // 2
    both = dot(table, b[0])
    return both[:rows] + (dot(table[:rows], b[1]) + both[rows:])


def lane_bit(shape, bit):
    return (lax.broadcasted_iota(jnp.int32, shape, 1) & bit) == 0


def gather_groups(parts, shape):
    for width in (16, 32, 64):
        first = lane_bit(shape, width)
        parts = [
            jnp.where(first, a, b) + pltpu.roll(jnp.where(first, b, a), width, 1)
            for a, b in zip(parts[0::2], parts[1::2])
        ]
    return parts[0]


def spread_groups(value, shape):
    parts = [value]
    for width in (64, 32, 16):
        first = lane_bit(shape, width)
        turned = [pltpu.roll(part, width, 1) for part in parts]
        parts = [
            side
            for part, turn in zip(parts, turned)
            for side in (jnp.where(first, part, turn), jnp.where(first, turn, part))
        ]
    return parts


def lines(ref, start):
    return jnp.concatenate([ref[pl.ds(row, PW, stride=BLK), :] for row in start], axis=0)


def source_masks():
    group = lax.broadcasted_iota(jnp.int32, (1, LANES), 1) // LB
    return [group == s for s in range(BD)]


def clear_kernel(unread, dense):
    zero = jnp.zeros((256, LANES), f32)

    def clear(i, carry):
        dense[pl.ds(pl.multiple_of(i * 256, 256), 256), :] = zero
        return carry

    lax.fori_loop(0, SLAB // 256, clear, 0)


def place_kernel(cells, *rest):
    blocks, (dense, turned) = rest[:HELD], rest[-2:]

    def turn(i, carry):
        at = pl.multiple_of(i * LANES, LANES)
        rows = [block[:, pl.ds(half * FIRST + at, LANES)] for half in range(2) for block in blocks]
        turned[pl.ds(at, LANES), :] = jnp.concatenate(rows, axis=0).T
        return carry

    lax.fori_loop(0, FIRST // LANES, turn, 0)
    masks = source_masks()

    def place(i, carry):
        for j in range(64):
            k = i * 64 + j
            row = turned[pl.ds(k, 1), :]
            for group in range(BD):
                half, p = group // HELD, group % HELD
                cell = cells[p * KW + half * FIRST + k]
                pltpu.store(dense.at[pl.ds(cell, 1), :], row, mask=masks[group])
        return carry

    lax.fori_loop(0, FIRST // 64, place, 0)


def fold_kernel(cells, *rest):
    given, zt, mh, ml, dense, sent0, sent1, turned, fields, high, low = rest[HELD:]
    place_kernel(cells, *rest[:HELD], dense, turned)
    table = zt[...]

    def along_z(i, carry):
        y, quad = i // 3, i % 3
        folded = []
        for side in range(4):
            base = (y * G + (quad * 4 + side) * 8) * G
            tiles = []
            for r in range(0, G, 8):
                parts = [dense[pl.ds(pl.multiple_of(base + xl * G + r, 8), 8), :] for xl in range(8)]
                tiles.append(gather_groups(parts, (8, LANES)))
            folded.append(jnp.concatenate(tiles, axis=0))
        out = transform(table, split(jnp.concatenate(folded, axis=1)))
        at = pl.multiple_of(y * G, G)
        for side in range(4):
            fields[quad * 4 + side, pl.ds(at, G), :] = out[:, side * LANES : (side + 1) * LANES]
        return carry

    lax.fori_loop(0, GY * 3, along_z, 0)

    def twelve(i, carry):
        at = pl.multiple_of(i * 16, 16)
        e = [fields[xh, pl.ds(at, 16), :] for xh in range(12)]
        c = cos12([e[0]] + [e[j] + e[12 - j] for j in range(1, 6)] + [e[6]])
        s = sin12([None] + [e[j] - e[12 - j] for j in range(1, 6)])
        for p in range(6):
            high[p, pl.ds(at, 16), :], low[p, pl.ds(at, 16), :] = split(
                jnp.concatenate([c[p], c[6] if p == 0 else s[p]], axis=1)
            )
        return carry

    lax.fori_loop(0, GY * G // 16, twelve, 0)
    for p in range(2 * PAIRS):
        out = dot3((high[p], low[p]), (mh[p], ml[p]))
        sent = (sent0, sent1)[p // PAIRS]
        for side in range(2):
            for y in range(GY):
                for z in range(GY):
                    at = y * G + z * PW
                    sent[pl.ds(y * COLS + z * XB + p % PAIRS * 2 + side, PW, stride=BLK), :] = out[
                        at : at + PW, side * LANES : (side + 1) * LANES
                    ]


def lane_of(shape, dim, half):
    wide = lax.broadcasted_iota(jnp.int32, shape, dim) // LB
    lane = lax.broadcasted_iota(jnp.int32, shape, 1 - dim)
    return jnp.where(wide + 64 * half == lane, 1.0, 0.0).astype(bf16)


def density_kernel(recv, yt, share, *rest):
    fields, sums = rest[-2:]
    table = yt[...]
    weight = share[...]
    first, second = [lane_of((WIDE, LANES), 0, half) for half in range(2)]

    def along_y(z, carry):
        data = [lines(recv, [y * COLS + z * XB + i for y in range(GY)]) for i in range(XB)]
        out = transform(table, split(jnp.concatenate(data, axis=1)))
        for i in range(XB):
            at = pl.multiple_of((z * XB + i) * G, G)
            fields[pl.ds(at, G), :] = out[:, i * LANES : (i + 1) * LANES]
        high, low = split(weight * out * out)
        added = dot(high[:HALF], first) + dot(low[:HALF], first)
        added = added + (dot(high[HALF:], second) + dot(low[HALF:], second))
        sums[pl.ds(pl.multiple_of(z * HALF, HALF), HALF), :] = added
        return carry

    lax.fori_loop(0, GY, along_y, 0)


def potential_kernel(density, external, fields, yt, sent):
    table = yt[...]
    first, second = [lane_of((LANES, WIDE), 1, half) for half in range(2)]

    def along_y(z, carry):
        at = pl.multiple_of(z * HALF, HALF)
        dens = density[pl.ds(at, HALF), :]
        root = jnp.exp(jnp.log(dens) * (1.0 / 3.0))
        root = root - (root - dens / (root * root)) * (1.0 / 3.0)
        high, low = split(external[pl.ds(at, HALF), :] - slater * root)
        spread = [dot(high, first) + dot(low, first), dot(high, second) + dot(low, second)]
        value = [fields[pl.ds(pl.multiple_of((z * XB + i) * G, G), G), :] for i in range(XB)]
        product = jnp.concatenate(spread, axis=0) * jnp.concatenate(value, axis=1)
        out = transform(table, split(product))
        for i in range(XB):
            for y in range(GY):
                sent[pl.ds(y * COLS + z * XB + i, PW, stride=BLK), :] = out[
                    y * PW : (y + 1) * PW, i * LANES : (i + 1) * LANES
                ]
        return carry

    lax.fori_loop(0, GY, along_y, 0)


def spread_kernel(recv0, recv1, zt, mh, ml, dense, uv, bh, bl):
    table = zt[...]
    for p in range(2 * PAIRS):
        recv = (recv0, recv1)[p // PAIRS]
        starts = [y * COLS + z * XB + p % PAIRS * 2 for y in range(GY) for z in range(GY)]
        data = [lines(recv, [row + side for row in starts]) for side in range(2)]
        uv[p] = dot3(split(jnp.concatenate(data, axis=1)), (mh[p], ml[p]))

    def twelve(i, carry):
        at = pl.multiple_of(i * 16, 16)
        left = [uv[p, pl.ds(at, 16), :LANES] for p in range(6)]
        right = [uv[p, pl.ds(at, 16), LANES:] for p in range(6)]
        c, s = cos12(left + [right[0]]), sin12([None] + right[1:])
        x = [c[0]] + [c[j] + s[j] for j in range(1, 6)] + [c[6]] + [c[j] - s[j] for j in range(5, 0, -1)]
        for quad in range(3):
            high, low = split(jnp.concatenate(x[4 * quad : 4 * quad + 4], axis=1))
            bh[quad, pl.ds(at, 16), :] = high
            bl[quad, pl.ds(at, 16), :] = low
        return carry

    lax.fori_loop(0, GY * G // 16, twelve, 0)

    def along_z(i, carry):
        y, quad = i // 3, i % 3
        at = pl.multiple_of(y * G, G)
        out = transform(table, (bh[quad, pl.ds(at, G), :], bl[quad, pl.ds(at, G), :]))
        for side in range(4):
            base = (y * G + (quad * 4 + side) * 8) * G
            for r in range(0, G, 8):
                copies = spread_groups(out[r : r + 8, side * LANES : (side + 1) * LANES], (8, LANES))
                for xl in range(8):
                    dense[pl.ds(pl.multiple_of(base + xl * G + r, 8), 8), :] = copies[xl]
        return carry

    lax.fori_loop(0, GY * 3, along_z, 0)


def pick_kernel(cells, dense, *rest):
    terms, turned = rest[-1 - HELD : -1], rest[-1]
    masks = source_masks()

    def pick(i, carry):
        for j in range(64):
            k = i * 64 + j
            row = None
            for group in range(BD):
                half, p = group // HELD, group % HELD
                value = dense[pl.ds(cells[p * KW + half * FIRST + k], 1), :]
                row = value if row is None else jnp.where(masks[group], value, row)
            turned[pl.ds(k, 1), :] = row
        return carry

    lax.fori_loop(0, FIRST // 64, pick, 0)

    def turn(i, carry):
        at = pl.multiple_of(i * LANES, LANES)
        rows = turned[pl.ds(at, LANES), :].T
        for group in range(BD):
            half, p = group // HELD, group % HELD
            terms[p][:, pl.ds(half * FIRST + at, LANES)] = rows[group * LB : (group + 1) * LB]
        return carry

    lax.fori_loop(0, FIRST // LANES, turn, 0)


def rotate_kernel(order, weights, coefs, *rest):
    blocks, rotated = rest[-1 - BD : -1], rest[-1]
    turned = split(weights[...].T)
    for at in range(0, KW, 512):
        part = pl.ds(at, 512)
        rotated[:, part] = dot3(turned, split(coefs[:, part]))
    for p in range(BD):
        blocks[p][...] = rotated[pl.ds(pl.multiple_of(order[p] * LB, LB), LB), :]


def pullback_kernel(grads, s, y0, y1, y2, y3, z1, z2, z3, z4, t1, t2, t3, t4, coefs, first, out):
    def mul(a, b):
        return dot3(split(a[...]), split(b[...]))

    y, z, t = (y0, y1, y2, y3), (None, z1, z2, z3, z4), (None, t1, t2, t3, t4)
    values = s[...]
    squared = jnp.sum(values * values, keepdims=True)
    frob = jnp.sqrt(squared)
    root = jnp.sqrt(frob)
    given = grads[...]
    zb = given / root
    fb = -0.5 * jnp.sum(given * z4[...], keepdims=True) / (frob * root)
    yb = None
    for k in range(NS_ITERS, 0, -1):
        tb = zb if k == 1 else mul(zb, z[k - 1])
        if yb is not None:
            tb = tb + mul(y[k - 1], yb)
        before = tb if k == 1 else mul(z[k - 1], tb)
        before = -0.5 * before
        if yb is not None:
            before = before + mul(yb, t[k])
        if k > 1:
            zb = mul(t[k], zb) - 0.5 * mul(tb, y[k - 1])
        yb = before
    fb = fb - jnp.sum(yb * values, keepdims=True) / squared
    grad = yb / frob + fb * (values / frob)
    both = split((grad + grad.T) / NPW)
    for at in range(0, KW, 512):
        part = pl.ds(at, 512)
        out[:, part] = first[:, part] + dot3(both, split(coefs[:, part]))


def dot_t(a, b):
    return lax.dot_general(a, b, (((1,), (1,)), ((), ())), preferred_element_type=f32)


def gram_kernel(coefs, out):
    equal = jnp.zeros((NB, NB), f32)
    mixed = jnp.zeros((NB, NB), f32)
    for at in range(0, KW, 512):
        high, low = split(coefs[:, pl.ds(at, 512)])
        equal = equal + dot_t(high, high)
        mixed = mixed + dot_t(high, low)
    out[...] = equal + (mixed + mixed.T)


def products_kernel(order, *rest):
    terms, rotated, (coefs, kinetic, occupancy, grads, sums) = rest[:BD], rest[BD : 2 * BD], rest[2 * BD :]
    for p in range(BD):
        rows = pl.ds(pl.multiple_of(order[p] * LB, LB), LB)
        grads[rows, :] = occupancy[rows, :] * (kinetic[...] * rotated[p][...] + terms[p][...])
    added = jnp.zeros((NB, NB), f32)
    for at in range(0, KW, 512):
        part = pl.ds(at, 512)
        a, b = split(coefs[:, part]), split(grads[:, part])
        added = added + (dot_t(a[0], b[0]) + (dot_t(a[0], b[1]) + dot_t(a[1], b[0])))
    sums[...] = added


def call(kernel, out_shapes, scratch, scalars, *operands, unread=(), alias=None, room=58, micros=3):
    vmem = pl.BlockSpec(memory_space=pltpu.VMEM)
    smem = pl.BlockSpec(memory_space=pltpu.SMEM)
    return pl.pallas_call(
        kernel,
        out_shape=out_shapes,
        in_specs=[smem] * scalars
        + [vmem] * (len(operands) - scalars)
        + [pl.BlockSpec(memory_space=pl.ANY)] * len(unread),
        out_specs=jax.tree.map(lambda _: vmem, out_shapes),
        scratch_shapes=scratch,
        input_output_aliases=alias or {},
        cost_estimate=pl.CostEstimate(flops=0, bytes_accessed=micros * 3_500_000, transcendentals=0),
        compiler_params=pltpu.CompilerParams(vmem_limit_bytes=room * 1024 * 1024),
    )(*operands, *unread)


def kept(*shape):
    return pltpu.VMEM(shape, f32)


def held(values):
    return pltpu.with_memory_space_constraint(values, pltpu.VMEM)


def array(*shape):
    return jax.ShapeDtypeStruct(shape, f32)


def matmul(left_side, right_side):
    return jnp.dot(left_side, right_side, precision=highest, preferred_element_type=f32)


def loewdin(intersection):
    frob_norm = jnp.sqrt(jnp.sum(intersection * intersection))
    identity = jnp.eye(intersection.shape[0], dtype=f32)
    ys, zs, ts = [intersection / frob_norm], [], []
    for repeat in range(NS_ITERS):
        product = matmul(zs[-1], ys[-1]) if zs else ys[-1]
        ts.append(1.5 * identity - 0.5 * product)
        zs.append(matmul(ts[-1], zs[-1]) if zs else ts[-1])
        if repeat < NS_ITERS - 1:
            ys.append(matmul(ys[-1], ts[-1]))
    return zs[-1] / jnp.sqrt(frob_norm), (*ys, *zs, *ts)


def total(values, beside=()):
    axes = ("pw", "band")
    pieces = lax.all_to_all(values, axes, split_axis=0, concat_axis=0, tiled=True)
    row = jnp.sum(pieces, axis=0, keepdims=True)
    row, *beside = lax.optimization_barrier((row, *beside))
    copies = jnp.broadcast_to(row, values.shape)
    return lax.all_to_all(copies, axes, split_axis=0, concat_axis=0, tiled=True), beside


def band_total(values):
    values = values + lax.ppermute(values, "band", [(i, i ^ 1) for i in range(BD)])
    others = [lax.ppermute(values, "band", [(i, (i + 2 * step) % BD) for i in range(BD)]) for step in (1, 2, 3)]
    return values + ((others[0] + others[2]) + others[1])


def packings():
    chosen = np.zeros((PARTS, 2, G, LANES), np.float32)
    for part in range(PARTS):
        blocks = [m for pair in BLOCKS[part * PAIRS : (part + 1) * PAIRS] for m in pair]
        for half in range(2):
            for i, m in enumerate(blocks):
                for q in range(BD):
                    chosen[part, half, m + 12 * q, half * 64 + i * BD + q] = 1
    return chosen


def to_sums(planes, chosen):
    values = planes.reshape(GY, 2, HALF, G)
    packed = matmul(values[:, 0], chosen[0]) + matmul(values[:, 1], chosen[1])
    return packed.reshape(SUM_ROWS, LANES)


def from_sums(parts, chosen):
    halves_of_y = [
        sum(matmul(parts[part], chosen[part, half].T) for part in range(PARTS)).reshape(GY, 1, HALF, G)
        for half in range(2)
    ]
    return jnp.concatenate(halves_of_y, axis=1).reshape(GY, G * G)


def shards(coefficients, occupancy, kinetic, cell_map, potential_ext, core_density):
    table = tables()
    chosen = packings()
    unused_lanes = (1.0 - chosen.sum(axis=(1, 2))).astype(np.float32)
    pw_pos = lax.axis_index("pw")
    band_pos = lax.axis_index("band")
    cells = cell_map - pw_pos * SLAB

    order = jnp.bitwise_xor(band_pos, jnp.asarray(ORDER, jnp.int32))
    cells = [lax.dynamic_slice_in_dim(cells, order[p] * KW, KW) for p in range(BD)]
    cells = [jnp.concatenate(cells[:HELD]), jnp.concatenate(cells[HELD:])]

    def meet(block, p):
        if ORDER[p] == 0:
            return block
        return lax.ppermute(block, "band", [(i, i ^ ORDER[p]) for i in range(BD)])

    intersection, planes = total(call(gram_kernel, array(NB, NB), [], 0, coefficients), (core_density, potential_ext))
    intersection = intersection / NPW
    core = [to_sums(planes[0], chosen[part]) + unused_lanes[part] for part in range(PARTS)]
    external = [to_sums(planes[1], chosen[part]) for part in range(PARTS)]
    weights, iterates = loewdin(intersection)
    rotated = call(
        rotate_kernel,
        [array(LB, KW)] * BD,
        [pltpu.VMEM((NB, KW), f32)],
        1,
        order,
        weights,
        coefficients,
        unread=(*cells, *core, *external),
        room=28,
    )
    near = [meet(rotated[p], p) for p in range(HELD)]
    dense = call(clear_kernel, kept(SLAB, LANES), [], 0, unread=(rotated[0],), room=28)
    *barred, dense = lax.optimization_barrier((*near, *rotated[HELD:], dense))
    blocks = [*barred[:HELD], *(meet(barred[p], p) for p in range(HELD, BD))]
    dense = call(
        place_kernel,
        kept(SLAB, LANES),
        [pltpu.VMEM((FIRST, LANES), f32)],
        1,
        cells[0],
        *blocks[:HELD],
        held(dense),
        alias={1 + HELD: 0},
        room=28,
        micros=14,
    )
    halves_shape = (2 * PAIRS, GY * G, 2 * LANES)
    unused, *sent = call(
        fold_kernel,
        (kept(SLAB, LANES), array(ROWS, LANES), array(ROWS, LANES)),
        [
            pltpu.VMEM((FIRST, LANES), f32),
            pltpu.VMEM((12, GY * G, LANES), f32),
            pltpu.VMEM(halves_shape, bf16),
            pltpu.VMEM(halves_shape, bf16),
        ],
        1,
        cells[1],
        *blocks[HELD:],
        held(dense),
        table["z_out"],
        *table["mix"],
        alias={1 + HELD: 0},
        room=28,
        micros=29,
    )
    *sent, kinetic, occupancy = lax.optimization_barrier((*sent, kinetic, occupancy))
    share = lax.dynamic_slice_in_dim(occupancy / NB, band_pos * LB, LB)
    share = jnp.tile(share, XB * BD).reshape(1, WIDE)
    kinetic_row = kinetic.reshape(1, KW)
    occupancy_column = occupancy.reshape(NB, 1)
    exchange = functools.partial(lax.all_to_all, axis_name="pw", split_axis=0, concat_axis=0, tiled=True)
    density, returned, after = [], [], []
    for part in range(PARTS):
        received = exchange(sent[part])
        fields, sums = call(
            density_kernel,
            (array(ROWS, LANES), array(SUM_ROWS, LANES)),
            [],
            0,
            received,
            table["y_out"],
            share,
            unread=after,
            room=28,
            micros=6,
        )
        density.append(core[part] + band_total(sums))
        product = call(
            potential_kernel,
            array(ROWS, LANES),
            [],
            0,
            density[part],
            external[part],
            fields,
            table["y_in"],
            room=28,
            micros=6,
        )
        after = [product]
        returned.append(exchange(product))
    dense = call(
        spread_kernel,
        kept(SLAB, LANES),
        [
            pltpu.VMEM((6, GY * G, 2 * LANES), f32),
            pltpu.VMEM((3, GY * G, 4 * LANES), bf16),
            pltpu.VMEM((3, GY * G, 4 * LANES), bf16),
        ],
        0,
        *returned,
        table["z_in"],
        *table["mix_t"],
        room=28,
        micros=13,
    )
    terms, after = [None, None], ()
    for side in (1, 0):
        terms[side] = call(
            pick_kernel,
            [array(LB, KW)] * HELD,
            [pltpu.VMEM((FIRST, LANES), f32)],
            1,
            cells[side],
            held(dense),
            unread=after,
            room=28,
            micros=14,
        )
        after = tuple(terms[side])
    far = [meet(terms[1][p], HELD + p) for p in range(HELD)]
    near = terms[0]
    barred = lax.optimization_barrier((*near, *far))
    near, far = barred[:HELD], barred[HELD:]
    terms = [meet(near[p], p) for p in range(HELD)] + list(far)
    grad_rotated, partial = call(
        products_kernel,
        (array(NB, KW), array(NB, NB)),
        [],
        1,
        order,
        *terms,
        *rotated,
        coefficients,
        kinetic_row,
        occupancy_column,
    )
    *density, partial = lax.optimization_barrier((*density, partial))
    grad_weights, unneeded = total(partial)
    first = matmul(weights, grad_rotated)
    grad_coef = call(
        pullback_kernel, array(NB, KW), [], 0, grad_weights, intersection, *iterates, coefficients, first
    )
    return (grad_coef, from_sums(density, chosen))


def solution(mesh):
    placed = (
        P(None, ("pw", "band")),
        P(),
        P(("pw", "band")),
        P("pw"),
        P("pw", None),
        P("pw", None),
    )
    return jax.shard_map(
        shards,
        mesh=mesh,
        in_specs=placed,
        out_specs=(P(None, ("pw", "band")), P("pw", None)),
        check_vma=False,
    )
```
